128 devices in a mesh: fsdp: 8 (over z_hi, x), tensor: 16 (over y, z_lo, core).
Axes of the slice: x: 4, y: 4, z: 4 (z_hi: 2, z_lo: 2; z = z_hi * 2 + z_lo), core: 2. Of those that a mesh axis runs over, the one named last changes fastest.
Arguments:
- iterate: bfloat16 [12800, 5120], P('fsdp', 'tensor'), may hold values from -0.0390625 to 0.0390625
Outputs:
- update: bfloat16 [12800, 5120], P('fsdp', 'tensor')
The draws below stay inside these ranges and needn't reach their ends.
All inputs are finite; a program needn't handle non-finite values.
Results may differ from the reference program's by a relative error of at most 0.0078.
Values may be sent and summed in bfloat16 or wider, within the bound.
A program may use at most 64 MiB of HBM per device.

```python
import jax
import jax.numpy as jnp
from jax import lax

ROWS = 12800
COLS = 5120


def level_of(own_key, extent, pieces, smallest, high):
    loudness, own = 1.0, jax.random.fold_in(own_key, 6)
    for axis_at, parts in pieces:
        draws = jnp.exp(jax.random.uniform(jax.random.fold_in(own, axis_at), (parts,), jnp.float32, smallest / len(pieces), high / len(pieces)))
        loudness = loudness * jnp.repeat(draws, extent[axis_at] // parts).reshape([-1 if axis == axis_at else 1 for axis in range(len(extent))])
    return loudness


def noise(rng, shape, spread, bound, split=(), kind=jnp.bfloat16):
    result = spread * jax.random.normal(rng, shape, jnp.float32)
    if split:
        result = result * level_of(rng, shape, split, -0.22, 0.18)
    return jnp.clip(result, -bound, bound).astype(kind)


def setup_inputs(seed: int = 0) -> dict:
    key_of = jax.random.split(jax.random.key(seed), 2)
    iterate = noise(key_of[0], (ROWS, COLS), (2 * ROWS) ** -0.5, 0.0390625, ((0, 8), (1, 16)))
    return {"iterate": iterate}


def reference(iterate):
    wide = iterate.astype(jnp.float32)
    gram = jnp.dot(wide.T, wide, precision=lax.Precision.HIGHEST)
    gram_b = gram.astype(jnp.bfloat16).astype(jnp.float32)
    first = jnp.dot(wide, gram_b, precision=lax.Precision.HIGHEST).astype(jnp.bfloat16)
    second = jnp.dot(first.astype(jnp.float32), gram_b, precision=lax.Precision.HIGHEST)
    factor = 0.2 * (ROWS ** 0.5)
    combined = 3.4445 * wide - 4.7750 * first.astype(jnp.float32) + 2.0315 * second
    return (factor * combined).astype(jnp.bfloat16)
```

```python
import jax
import jax.numpy as jnp
from jax import lax
from jax.sharding import PartitionSpec as P

ROWS = 12800


def transposed_product(left, right):
    return lax.dot_general(
        left, right, (((0,), (0,)), ((), ())), preferred_element_type=jnp.float32
    )


def shards(iterate):
    gathered = lax.all_gather(iterate, "tensor", axis=1, tiled=True)
    partial = transposed_product(gathered, iterate).astype(jnp.bfloat16)
    block = lax.psum_scatter(partial, "fsdp", scatter_dimension=0, tiled=True)
    columns = lax.all_gather(block, "fsdp", axis=0, tiled=True)
    rows = lax.all_gather(block, "tensor", axis=1, tiled=True)
    square = jnp.dot(rows, columns, preferred_element_type=jnp.float32)
    poly = (2.0315 * square - 4.775 * block.astype(jnp.float32)).astype(jnp.bfloat16)
    panel = lax.all_gather(poly, "fsdp", axis=0, tiled=True)
    product = jnp.dot(gathered, panel, preferred_element_type=jnp.float32)
    factor = 0.2 * ROWS**0.5
    return (factor * (3.4445 * iterate.astype(jnp.float32) + product)).astype(jnp.bfloat16)


def solution(mesh):
    placed = (P("fsdp", "tensor"),)
    return jax.shard_map(
        shards, mesh=mesh, in_specs=placed, out_specs=P("fsdp", "tensor"), check_vma=False
    )
```

```python
import functools

import jax
import jax.numpy as jnp
from jax import lax
from jax.experimental import pallas as pl
from jax.experimental.pallas import tpu as pltpu
from jax.sharding import PartitionSpec as P

MESH = pl.DeviceIdType.MESH
BF16, F32 = jnp.bfloat16, jnp.float32
ROWS = 12800
FACTOR = 0.2 * ROWS**0.5
A, B, C = 3.4445, -4.775, 2.0315


class Where:
    def __init__(self):
        f, t = lax.axis_index("fsdp"), lax.axis_index("tensor")
        self.zh, self.x = f // 4, f % 4
        self.y, self.zl, self.c = t // 4, (t // 2) % 2, t % 2

    def device(self, dx=0, dzh=0, dy=0, dzl=0, dc=0):
        x, y = (self.x + dx) % 4, (self.y + dy) % 4
        zh, zl, c = (self.zh + dzh) % 2, (self.zl + dzl) % 2, (self.c + dc) % 2
        return (zh * 4 + x, y * 4 + zl * 2 + c)

    def tslot(self, d, dz):
        return (self.y + d) % 4 * 2 + (self.zl + dz) % 2

    def fslot(self, d, dz):
        return (self.x + d) % 4 * 2 + (self.zh + dz) % 2


class Gather:
    def __init__(self, view, slot, device, send, recv, twice):
        self.view, self.slot, self.device, self.send, self.recv = view, slot, device, send, recv
        ring_p, ring_m, pair = (1, 0), (-1, 0), (0, 1)
        if twice:
            self.plan = {
                "ap": ((0, 0), ring_p, None), "am": ((0, 0), ring_m, None), "az": ((0, 0), pair, None),
                "bm": ((1, 0), ring_m, None), "bz": ((1, 0), pair, None), "bp": ((0, 1), ring_p, None),
                "cp": ((-1, 1), ring_p, 0), "cm": ((1, 1), ring_m, 1),
            }
            self.after = {"am": ("bm", "bz"), "az": ("bp",), "bp": ("cp",), "bz": ("cm",)}
            self.order = [("az",), ("am",), ("ap",), ("bp",), ("bz",), ("bm",), ("cp", "cm")]
        else:
            self.plan = {
                "ap": ((0, 0), ring_p, None), "am": ((0, 0), ring_m, None), "az": ((0, 0), pair, None),
                "bp": ((0, 1), ring_p, None), "bm": ((0, 1), ring_m, None),
                "cp": ((-1, 0), ring_p, 0), "cm": ((1, 0), ring_m, 1),
                "dp": ((-1, 1), ring_p, 0), "dm": ((1, 1), ring_m, 1),
            }
            self.after = {"az": ("bp", "bm"), "ap": ("cp",), "am": ("cm",), "bp": ("dp",), "bm": ("dm",)}
            self.order = [("az",), ("ap",), ("am",), ("bp",), ("bm",), ("cp", "cm"), ("dp", "dm")]
        self.names = list(self.plan)

    def copy(self, name, receiving):
        (d, dz), (step, flip), half = self.plan[name]
        if receiving:
            d, dz = d - step, (dz + flip) % 2
        i = self.names.index(name)
        ref = self.view(self.slot(d, dz), half)
        return pltpu.make_async_remote_copy(
            src_ref=ref, dst_ref=ref, send_sem=self.send.at[i], recv_sem=self.recv.at[i],
            device_id=self.device(step, flip), device_id_type=MESH,
        )

    def start(self, name):
        self.copy(name, False).start()

    def begin(self):
        for name in ("az", "am", "ap"):
            self.start(name)

    def take(self, names):
        for name in names:
            self.copy(name, True).wait_recv()
            for nxt in self.after.get(name, ()):
                self.start(nxt)
        (d, dz), (step, flip), _ = self.plan[names[0]]
        return d - step, (dz + flip) % 2

    def end(self):
        for name in self.names:
            self.copy(name, False).wait_send()


def kernel(
    x_ref, o_ref, xin, xb, gp, crecv, own, rsst, rsrecv, rzst, rzrecv, ga, gc, pc, acc, uo, urecv,
    ts, tr, gs, gr, hs, hr, ps, pr, xs, xr, cs, cr, rss, rsr, zs, zr, shs, shr, pss, psr, us, ur,
):
    w = Where()
    c = w.c
    rows, width = x_ref.shape
    half, full = rows // 2, 2 * width
    mate = w.device(dc=1)

    peers = [dict(dc=1), dict(dy=1), dict(dy=-1), dict(dzl=1), dict(dx=1), dict(dx=-1), dict(dx=2), dict(dzh=1)]
    barrier = pltpu.get_barrier_semaphore()
    for peer in peers:
        pl.semaphore_signal(barrier, inc=1, device_id=w.device(**peer), device_id_type=MESH)
    pl.semaphore_wait(barrier, len(peers))

    def remote(src, dst, send, recv, device):
        return pltpu.make_async_remote_copy(
            src_ref=src, dst_ref=dst, send_sem=send, recv_sem=recv, device_id=device, device_id_type=MESH
        )

    swap = remote(x_ref.at[pl.ds((1 - c) * half, half), :], xin, xs, xr, mate)
    swap.start()
    mine = w.tslot(0, 0)
    swap.wait_recv()
    step_rows = half // 5

    def join(i, _):
        at = pl.ds(i * step_rows, step_rows)
        kept, got = x_ref[pl.ds(c * half + i * step_rows, step_rows), :], xin[at, :]
        first = c == 0
        xb[mine, at, :] = jnp.concatenate([jnp.where(first, kept, got), jnp.where(first, got, kept)], axis=1)
        return 0

    lax.fori_loop(0, 5, join, 0)

    def tdevice(step, flip):
        return w.device(dy=step, dzl=flip)

    def fdevice(step, flip):
        return w.device(dx=step, dzh=flip)

    def xview(slot, part):
        if part is None:
            return xb.at[slot]
        return xb.at[slot, pl.ds(part * (half // 2), half // 2), :]

    gx = Gather(xview, w.tslot, tdevice, ts, tr, True)
    gx.begin()
    kept_rows = pl.ds(c * width, width)
    other_rows = pl.ds((1 - c) * width, width)

    def gram(step, rel):
        slot = w.tslot(*rel)
        buf = step % 2

        def tile(i, _):
            at = pl.ds(pl.multiple_of(i * 128, 128), 128)
            gp[buf, at, :] = lax.dot_general(
                xb[slot, :, at], xb[mine], (((0,), (0,)), ((), ())), preferred_element_type=F32
            )
            return 0

        lax.fori_loop(0, full // 128, tile, 0)
        remote(gp.at[buf, other_rows, :], crecv.at[step], cs.at[step], cr.at[step], mate).start()

    def scatter(step, rel):
        buf = step % 2
        cp = remote(gp.at[buf, other_rows, :], crecv.at[step], cs.at[step], cr.at[step], mate)
        cp.wait_recv()
        total = gp[buf, kept_rows, :] + crecv[step]
        cp.wait_send()
        to_x, to_zh = (w.y + rel[0]) % 4, (w.zl + rel[1]) % 2
        away = (to_x - w.x + 4) % 4

        @pl.when(away == 0)
        def _():
            own[to_zh] = total

        @pl.when(away != 0)
        def _():
            rsst[step] = total.astype(BF16)
            remote(
                rsst.at[step], rsrecv.at[to_zh, away - 1], rss.at[step], rsr.at[to_zh, away - 1],
                w.device(dx=away),
            ).start()

    steps = [(0, 0)]
    gram(0, (0, 0))
    for names in gx.order:
        rel = gx.take(names)
        gram(len(steps), rel)
        scatter(len(steps) - 1, steps[-1])
        steps.append(rel)
    scatter(7, steps[-1])

    def received(zh):
        for i in range(3):
            remote(rsst.at[0], rsrecv.at[zh, i], rss.at[0], rsr.at[zh, i], mate).wait_recv()
        return own[zh] + rsrecv[zh, 0].astype(F32) + rsrecv[zh, 1].astype(F32) + rsrecv[zh, 2].astype(F32)

    across = remote(rzst, rzrecv, zs, zr, w.device(dzh=1))
    rzst[...] = received(1 - w.zh).astype(BF16)
    across.start()
    own[w.zh] = received(w.zh)
    across.wait_recv()
    block = (own[w.zh] + rzrecv[...].astype(F32)).astype(BF16)

    fmine = w.fslot(0, 0)
    ga[mine] = block
    gc[fmine, kept_rows, :] = block

    def rows_of(buf):
        def view(slot, part):
            if part is None:
                return buf.at[slot, kept_rows, :]
            return buf.at[slot, pl.ds(c * width + part * (width // 2), width // 2), :]

        return view

    def aview(slot, part):
        if part is None:
            return ga.at[slot]
        return ga.at[slot, pl.ds(part * (width // 2), width // 2), :]

    def share(buf, slot, send, recv):
        ref = buf.at[slot, kept_rows, :]
        return remote(ref, ref, send.at[slot], recv.at[slot], mate)

    def shared(buf, slot, send, recv):
        ref = buf.at[slot, other_rows, :]
        return remote(ref, ref, send.at[slot], recv.at[slot], mate)

    ggc = Gather(rows_of(gc), w.fslot, fdevice, gs, gr, False)
    gga = Gather(aview, w.tslot, tdevice, hs, hr, True)
    ggc.begin()
    gga.begin()
    share(gc, fmine, shs, shr).start()
    for na, nc in zip(gga.order, ggc.order):
        gga.take(na)
        rel = ggc.take(nc)
        share(gc, w.fslot(*rel), shs, shr).start()
    for j in range(8):
        shared(gc, j, shs, shr).wait_recv()

    def square(j, total):
        return total + jnp.dot(ga[j], gc[j], preferred_element_type=F32)

    total = lax.fori_loop(0, 8, square, jnp.zeros((width, full), F32))
    pc[fmine, kept_rows, :] = (C * total + B * ga[mine].astype(F32)).astype(BF16)

    gpc = Gather(rows_of(pc), w.fslot, fdevice, ps, pr, True)
    gpc.begin()
    share(pc, fmine, pss, psr).start()
    tile_rows = half // 5

    def product(slot, first):
        shared(pc, slot, pss, psr).wait_recv()

        def tile(i, _):
            at = pl.ds(pl.multiple_of(i * tile_rows, tile_rows), tile_rows)
            term = jnp.dot(xb[slot, at, :], pc[slot], preferred_element_type=F32)
            if first:
                acc[at, :] = A * xb[mine, at, :].astype(F32) + term
            else:
                acc[at, :] += term
            return 0

        lax.fori_loop(0, 5, tile, 0)

    waiting = fmine
    for i, names in enumerate(gpc.order):
        rel = gpc.take(names)
        slot = w.fslot(*rel)
        share(pc, slot, pss, psr).start()
        product(waiting, i == 0)
        waiting = slot
    product(waiting, False)

    back = remote(uo, urecv, us, ur, mate)

    def split(i, _):
        at = pl.ds(pl.multiple_of(i * tile_rows, tile_rows), tile_rows)
        value = (FACTOR * acc[at, :]).astype(BF16)
        left, right = value[:, :width], value[:, width:]
        first = c == 0
        o_ref[pl.ds(pl.multiple_of(c * half + i * tile_rows, 16), tile_rows), :] = jnp.where(first, left, right)
        uo[at, :] = jnp.where(first, right, left)
        return 0

    lax.fori_loop(0, 5, split, 0)
    back.start()

    swap.wait_send()
    for g in (gx, ggc, gga, gpc):
        g.end()
    for i, rel in enumerate(steps):
        away = ((w.y + rel[0]) % 4 - w.x + 4) % 4

        @pl.when(away != 0)
        def _():
            remote(rsst.at[i], rsrecv.at[0, 0], rss.at[i], rsr.at[0, 0], mate).wait_send()

    across.wait_send()
    for j in range(8):
        share(gc, j, shs, shr).wait_send()
        share(pc, j, pss, psr).wait_send()
    back.wait()
    o_ref[pl.ds((1 - c) * half, half), :] = urecv[...]


def shards(iterate):
    rows, width = iterate.shape
    half, full = rows // 2, 2 * width
    dma = pltpu.SemaphoreType.DMA
    vmem = pltpu.VMEM
    return pl.pallas_call(
        kernel,
        out_shape=jax.ShapeDtypeStruct((rows, width), BF16),
        in_specs=[pl.BlockSpec(memory_space=pltpu.VMEM)],
        out_specs=pl.BlockSpec(memory_space=pltpu.VMEM),
        scratch_shapes=[
            vmem((half, width), BF16),
            vmem((8, half, full), BF16),
            vmem((2, full, full), F32),
            vmem((8, width, full), F32),
            vmem((2, width, full), F32),
            vmem((8, width, full), BF16),
            vmem((2, 3, width, full), BF16),
            vmem((width, full), BF16),
            vmem((width, full), BF16),
            vmem((8, width, full), BF16),
            vmem((8, full, full), BF16),
            vmem((8, full, full), BF16),
            vmem((half, full), F32),
            vmem((half, width), BF16),
            vmem((half, width), BF16),
            dma((8,)), dma((8,)), dma((9,)), dma((9,)), dma((8,)), dma((8,)), dma((8,)), dma((8,)),
            dma, dma, dma((8,)), dma((8,)), dma((8,)), dma((2, 3)), dma, dma,
            dma((8,)), dma((8,)), dma((8,)), dma((8,)), dma, dma,
        ],
        compiler_params=pltpu.CompilerParams(
            collective_id=0, has_side_effects=True, vmem_limit_bytes=60 * 2**20
        ),
        cost_estimate=pl.CostEstimate(flops=6 * rows * width * 16 * width, bytes_accessed=4 * rows * width, transcendentals=0),
        name="newton_schulz",
    )(iterate)


def solution(mesh):
    return jax.shard_map(
        shards, mesh=mesh, in_specs=(P("fsdp", "tensor"),), out_specs=P("fsdp", "tensor"), check_vma=False
    )
```

```python
import functools

import jax
import jax.numpy as jnp
from jax import lax
from jax.experimental import pallas as pl
from jax.experimental.pallas import tpu as pltpu
from jax.sharding import PartitionSpec as P

MESH = pl.DeviceIdType.MESH
BF16, F32 = jnp.bfloat16, jnp.float32
ROWS = 12800
FACTOR = 0.2 * ROWS**0.5
A, B, C = 3.4445, -4.775, 2.0315
X_CHUNKS, G_CHUNKS = 1, 1


class Where:
    def __init__(self):
        f, t = lax.axis_index("fsdp"), lax.axis_index("tensor")
        self.zh, self.x = f // 4, f % 4
        self.y, self.zl, self.c = t // 4, (t // 2) % 2, t % 2

    def device(self, dx=0, dzh=0, dy=0, dzl=0, dc=0):
        x, y = (self.x + dx) % 4, (self.y + dy) % 4
        zh, zl, c = (self.zh + dzh) % 2, (self.zl + dzl) % 2, (self.c + dc) % 2
        return (zh * 4 + x, y * 4 + zl * 2 + c)

    def tslot(self, d, dz):
        return (self.y + d) % 4 * 2 + (self.zl + dz) % 2

    def fplace(self, d, dz):
        return (self.x + d) % 4, (self.zh + dz) % 2


class Gather:
    def __init__(self, chunks, view, slot, device, send, recv, twice):
        self.chunks, self.view, self.slot, self.device, self.send, self.recv = chunks, view, slot, device, send, recv
        ring_p, ring_m, pair = (1, 0), (-1, 0), (0, 1)
        if twice:
            self.plan = {
                "ap": ((0, 0), ring_p, None), "am": ((0, 0), ring_m, None), "az": ((0, 0), pair, None),
                "bm": ((1, 0), ring_m, None), "bz": ((1, 0), pair, None), "bp": ((0, 1), ring_p, None),
                "cp": ((-1, 1), ring_p, 0), "cm": ((1, 1), ring_m, 1),
            }
            self.after = {"am": ("bm", "bz"), "az": ("bp",), "bp": ("cp",), "bz": ("cm",)}
            self.order = [("az",), ("am",), ("ap",), ("bp",), ("bz",), ("bm",), ("cp", "cm")]
        else:
            self.plan = {
                "ap": ((0, 0), ring_p, None), "am": ((0, 0), ring_m, None), "az": ((0, 0), pair, None),
                "bp": ((0, 1), ring_p, None), "bm": ((0, 1), ring_m, None),
                "cp": ((-1, 0), ring_p, 0), "cm": ((1, 0), ring_m, 1),
                "dp": ((-1, 1), ring_p, 0), "dm": ((1, 1), ring_m, 1),
            }
            self.after = {"az": ("bp", "bm"), "ap": ("cp",), "am": ("cm",), "bp": ("dp",), "bm": ("dm",)}
            self.order = [("az",), ("ap",), ("am",), ("bp",), ("bm",), ("cp", "cm"), ("dp", "dm")]
        self.names = list(self.plan)

    def copy(self, name, chunk, receiving):
        (d, dz), (step, flip), part = self.plan[name]
        if receiving:
            d, dz = d - step, (dz + flip) % 2
        i = self.names.index(name)
        ref = self.view(self.slot(d, dz), chunk, part)
        return pltpu.make_async_remote_copy(
            src_ref=ref, dst_ref=ref, send_sem=self.send.at[chunk, i], recv_sem=self.recv.at[chunk, i],
            device_id=self.device(step, flip), device_id_type=MESH,
        )

    def begin(self):
        for chunk in range(self.chunks):
            for name in ("az", "am", "ap"):
                self.copy(name, chunk, False).start()

    def take(self, names):
        for chunk in range(self.chunks):
            for name in names:
                self.copy(name, chunk, True).wait_recv()
                for nxt in self.after.get(name, ()):
                    self.copy(nxt, chunk, False).start()
        (d, dz), (step, flip), _ = self.plan[names[0]]
        return d - step, (dz + flip) % 2

    def end(self):
        for chunk in range(self.chunks):
            for name in self.names:
                self.copy(name, chunk, False).wait_send()


def kernel(
    x_ref, o_ref, xin, xb, gp, crecv, own, rsst, rsrecv, rzst, rzrecv, ga, gc, pc, acc, uo, urecv,
    ts, tr, gs, gr, hs, hr, ps, pr, xs, xr, cs, cr, rss, rsr, zs, zr, shs, shr, pss, psr, us, ur,
):
    w = Where()
    c = w.c
    rows, width = x_ref.shape
    half, full, quarter = rows // 2, 2 * width, width // 4
    mate = w.device(dc=1)

    peers = [dict(dc=1), dict(dy=1), dict(dy=-1), dict(dzl=1), dict(dx=1), dict(dx=-1), dict(dx=2), dict(dzh=1)]
    barrier = pltpu.get_barrier_semaphore()
    for peer in peers:
        pl.semaphore_signal(barrier, inc=1, device_id=w.device(**peer), device_id_type=MESH)
    pl.semaphore_wait(barrier, len(peers))

    def remote(src, dst, send, recv, device):
        return pltpu.make_async_remote_copy(
            src_ref=src, dst_ref=dst, send_sem=send, recv_sem=recv, device_id=device, device_id_type=MESH
        )

    swap = remote(x_ref.at[pl.ds((1 - c) * half, half), :], xin, xs, xr, mate)
    swap.start()
    mine = w.tslot(0, 0)
    swap.wait_recv()
    step_rows = half // 5

    def join(i, _):
        at = pl.ds(i * step_rows, step_rows)
        kept, got = x_ref[pl.ds(c * half + i * step_rows, step_rows), :], xin[at, :]
        first = c == 0
        xb[mine, at, :] = jnp.concatenate([jnp.where(first, kept, got), jnp.where(first, got, kept)], axis=1)
        return 0

    lax.fori_loop(0, 5, join, 0)

    def tdevice(step, flip):
        return w.device(dy=step, dzl=flip)

    def fdevice(step, flip):
        return w.device(dx=step, dzh=flip)

    chunk_rows = half // X_CHUNKS
    part_rows = (chunk_rows // 32 + 1) * 16

    def xview(slot, chunk, part):
        at, size = ((0, chunk_rows), (0, part_rows), (part_rows, chunk_rows - part_rows))[0 if part is None else part + 1]
        return xb.at[slot, pl.ds(chunk * chunk_rows + at, size), :]

    gx = Gather(X_CHUNKS, xview, w.tslot, tdevice, ts, tr, True)
    gx.begin()
    kept_rows = pl.ds(c * width, width)
    other_rows = pl.ds((1 - c) * width, width)

    def gram(step, rel):
        slot = w.tslot(*rel)
        buf = step % 2

        gp[buf] = lax.dot_general(xb[slot], xb[mine], (((0,), (0,)), ((), ())), preferred_element_type=F32)
        remote(gp.at[buf, other_rows, :], crecv.at[step], cs.at[step], cr.at[step], mate).start()

    def scatter(step, rel):
        buf = step % 2
        cp = remote(gp.at[buf, other_rows, :], crecv.at[step], cs.at[step], cr.at[step], mate)
        cp.wait_recv()
        total = gp[buf, kept_rows, :] + crecv[step]
        cp.wait_send()
        own[w.tslot(*rel)] = gp_quarter(buf, step)
        rsst[step] = total.astype(BF16)
        for d in (1, 2, 3):
            x_copy(step, rel, d).start()

    def gp_quarter(buf, step):
        return gp[buf, pl.ds(c * width + w.x * quarter, quarter), :] + crecv[step, pl.ds(w.x * quarter, quarter), :]

    def x_copy(step, rel, d):
        to = (w.x + d) % 4
        slot = w.tslot(*rel)
        return remote(
            rsst.at[step, pl.ds(to * quarter, quarter), :], rsrecv.at[d - 1, slot],
            rss.at[step, d - 1], rsr.at[d - 1, slot], w.device(dx=d),
        )

    def z_copy(rel):
        at = (w.y + rel[0]) % 4
        return remote(rzst.at[at], rzrecv.at[at], zs.at[at], zr.at[at], w.device(dzh=1))

    def summed(step, rel):
        slot = w.tslot(*rel)
        for d in (1, 2, 3):
            x_copy(step, rel, d).wait_recv()
        total = own[slot] + sum(rsrecv[d, slot].astype(F32) for d in range(3))
        there = (w.zl + rel[1]) % 2 != w.zh

        @pl.when(there)
        def _():
            rzst[(w.y + rel[0]) % 4] = total.astype(BF16)
            z_copy(rel).start()

        @pl.when(jnp.logical_not(there))
        def _():
            own[slot] = total

    steps = [(0, 0)]
    gram(0, (0, 0))
    for names in gx.order:
        rel = gx.take(names)
        gram(len(steps), rel)
        scatter(len(steps) - 1, steps[-1])
        if len(steps) > 2:
            summed(len(steps) - 3, steps[-3])
        steps.append(rel)
    scatter(7, steps[-1])
    for i in (5, 6, 7):
        summed(i, steps[i])

    kept_quarter = pl.ds(c * width + w.x * quarter, quarter)
    for i in range(4):
        z_copy((i, w.zh - w.zl + 2)).wait_recv()
        at = (w.y + i) % 4
        block = (own[at * 2 + w.zh] + rzrecv[at].astype(F32)).astype(BF16)
        ga[mine, at] = block
        gc[at, w.zh, kept_quarter, :] = block

    def which_of(chunk, part):
        size = 4 // G_CHUNKS
        return (chunk * size, size) if part is None else (chunk * size + part * (size // 2), size // 2)

    def rows_of(buf):
        def view(place, chunk, part):
            x, zh = place
            which = pl.ds(*which_of(chunk, part))
            return buf.at[which, zh, pl.ds(c * width + x * quarter, quarter), :]

        return view

    def aview(slot, chunk, part):
        return ga.at[slot, pl.ds(*which_of(chunk, part))]

    def share(buf, place, send, recv):
        x, zh = place
        ref = buf.at[:, zh, pl.ds(c * width + x * quarter, quarter), :]
        return remote(ref, ref, send.at[x * 2 + zh], recv.at[x * 2 + zh], mate)

    def shared(buf, place, send, recv):
        x, zh = place
        ref = buf.at[:, zh, pl.ds((1 - c) * width + x * quarter, quarter), :]
        return remote(ref, ref, send.at[x * 2 + zh], recv.at[x * 2 + zh], mate)

    fmine = w.fplace(0, 0)
    ggc = Gather(G_CHUNKS, rows_of(gc), w.fplace, fdevice, gs, gr, False)
    gga = Gather(G_CHUNKS, aview, w.tslot, tdevice, hs, hr, True)
    ggc.begin()
    gga.begin()
    share(gc, fmine, shs, shr).start()
    for na, nc in zip(gga.order, ggc.order):
        gga.take(na)
        rel = ggc.take(nc)
        share(gc, w.fplace(*rel), shs, shr).start()
    for j in range(8):
        shared(gc, (j // 2, j % 2), shs, shr).wait_recv()

    total = jnp.dot(
        jnp.concatenate([ga[j].reshape(width, full) for j in range(8)], axis=1),
        gc[...].reshape(8 * full, full), preferred_element_type=F32,
    )
    value = (C * total + B * ga[mine].reshape(width, full).astype(F32)).astype(BF16)
    for i in range(4):
        pc[i, w.zh, kept_quarter, :] = value[i * quarter:(i + 1) * quarter]

    gpc = Gather(G_CHUNKS, rows_of(pc), w.fplace, fdevice, ps, pr, True)
    gpc.begin()
    share(pc, fmine, pss, psr).start()
    tile_rows = half // 5

    def product(zh, first):
        for x in range(4):
            shared(pc, (x, zh), pss, psr).wait_recv()

        left = jnp.concatenate([xb[j * 2 + zh] for j in range(4)], axis=1)
        for at in range(0, full, 256):
            cols = pl.ds(at, min(256, full - at))
            right = jnp.concatenate([pc[j, zh, :, cols] for j in range(4)], axis=0)
            start = A * xb[mine, :, cols].astype(F32) if first else acc[:, cols]
            acc[:, cols] = start + jnp.dot(left, right, preferred_element_type=F32)

    for names in gpc.order:
        if names == ("cp", "cm"):
            product(w.zh, True)
        share(pc, w.fplace(*gpc.take(names)), pss, psr).start()
    product(1 - w.zh, False)

    back = remote(uo, urecv, us, ur, mate)

    def split(i, _):
        at = pl.ds(pl.multiple_of(i * tile_rows, tile_rows), tile_rows)
        value = (FACTOR * acc[at, :]).astype(BF16)
        left, right = value[:, :width], value[:, width:]
        first = c == 0
        o_ref[pl.ds(pl.multiple_of(c * half + i * tile_rows, 16), tile_rows), :] = jnp.where(first, left, right)
        uo[at, :] = jnp.where(first, right, left)
        return 0

    lax.fori_loop(0, 5, split, 0)
    back.start()

    swap.wait_send()
    for g in (gx, ggc, gga, gpc):
        g.end()
    for i, rel in enumerate(steps):
        for d in (1, 2, 3):
            x_copy(i, rel, d).wait_send()
    for i in range(4):
        z_copy((i, 0)).wait_send()
    for j in range(8):
        share(gc, (j // 2, j % 2), shs, shr).wait_send()
        share(pc, (j // 2, j % 2), pss, psr).wait_send()
    back.wait()
    o_ref[pl.ds((1 - c) * half, half), :] = urecv[...]


def shards(iterate):
    rows, width = iterate.shape
    half, full, quarter = rows // 2, 2 * width, width // 4
    dma = pltpu.SemaphoreType.DMA
    vmem = pltpu.VMEM
    return pl.pallas_call(
        kernel,
        out_shape=jax.ShapeDtypeStruct((rows, width), BF16),
        in_specs=[pl.BlockSpec(memory_space=pltpu.VMEM)],
        out_specs=pl.BlockSpec(memory_space=pltpu.VMEM),
        scratch_shapes=[
            vmem((half, width), BF16),
            vmem((8, half, full), BF16),
            vmem((2, full, full), F32),
            vmem((8, width, full), F32),
            vmem((8, quarter, full), F32),
            vmem((8, width, full), BF16),
            vmem((3, 8, quarter, full), BF16),
            vmem((4, quarter, full), BF16),
            vmem((4, quarter, full), BF16),
            vmem((8, 4, quarter, full), BF16),
            vmem((4, 2, full, full), BF16),
            vmem((4, 2, full, full), BF16),
            vmem((half, full), F32),
            vmem((half, width), BF16),
            vmem((half, width), BF16),
            dma((X_CHUNKS, 8)), dma((X_CHUNKS, 8)), dma((G_CHUNKS, 9)), dma((G_CHUNKS, 9)),
            dma((G_CHUNKS, 8)), dma((G_CHUNKS, 8)), dma((G_CHUNKS, 8)), dma((G_CHUNKS, 8)),
            dma, dma, dma((8,)), dma((8,)), dma((8, 3)), dma((3, 8)), dma((4,)), dma((4,)),
            dma((8,)), dma((8,)), dma((8,)), dma((8,)), dma, dma,
        ],
        compiler_params=pltpu.CompilerParams(
            collective_id=0, has_side_effects=True, vmem_limit_bytes=60 * 2**20
        ),
        cost_estimate=pl.CostEstimate(flops=6 * rows * width * 16 * width, bytes_accessed=4 * rows * width, transcendentals=0),
        name="newton_schulz",
    )(iterate)


def solution(mesh):
    return jax.shard_map(
        shards, mesh=mesh, in_specs=(P("fsdp", "tensor"),), out_specs=P("fsdp", "tensor"), check_vma=False
    )
```

```python
import functools

import jax
import jax.numpy as jnp
from jax import lax
from jax.experimental import pallas as pl
from jax.experimental.pallas import tpu as pltpu
from jax.sharding import PartitionSpec as P

MESH = pl.DeviceIdType.MESH
BF16, F32 = jnp.bfloat16, jnp.float32
ROWS = 12800
FACTOR = 0.2 * ROWS**0.5
A, B, C = 3.4445, -4.775, 2.0315
GP = 4


class Where:
    def __init__(self):
        f, t = lax.axis_index("fsdp"), lax.axis_index("tensor")
        self.zh, self.x = f // 4, f % 4
        self.y, self.zl, self.c = t // 4, (t // 2) % 2, t % 2

    def device(self, dx=0, dzh=0, dy=0, dzl=0, dc=0):
        x, y = (self.x + dx) % 4, (self.y + dy) % 4
        zh, zl, c = (self.zh + dzh) % 2, (self.zl + dzl) % 2, (self.c + dc) % 2
        return (zh * 4 + x, y * 4 + zl * 2 + c)

    def tplace(self, d, dz):
        return (self.y + d) % 4, (self.zl + dz) % 2

    def fplace(self, d, dz):
        return (self.x + d) % 4, (self.zh + dz) % 2


OWN, MINUS, PLUS, OTHER = (0, 0), (-1, 0), (1, 0), (0, 1)
FIRST = {"az": (OWN, (0, 1), None), "ap": (OWN, (1, 0), None), "am": (OWN, (-1, 0), None)}
TWICE = (
    FIRST | {
        "bm": (PLUS, (-1, 0), None), "bz": (PLUS, (0, 1), None), "bp": (OTHER, (1, 0), None),
        "cp": ((-1, 1), (1, 0), 0), "cm": ((1, 1), (-1, 0), 1),
    },
    {"am": ("bm", "bz"), "az": ("bp",), "bp": ("cp",), "bz": ("cm",)},
    [("az",), ("am",), ("ap",), ("bp",), ("bz",), ("bm",), ("cp", "cm")],
)
ONCE = (
    FIRST | {
        "bp": (OTHER, (1, 0), None), "bm": (OTHER, (-1, 0), None), "cp": (MINUS, (1, 0), 0), "cm": (PLUS, (-1, 0), 1),
        "dp": ((-1, 1), (1, 0), 0), "dm": ((1, 1), (-1, 0), 1),
    },
    {"az": ("bp", "bm"), "ap": ("cp",), "am": ("cm",), "bp": ("dp",), "bm": ("dm",)},
    [("az",), ("ap",), ("am",), ("bp",), ("bm",), ("cp", "cm"), ("dp", "dm")],
)
DIRECT = (
    FIRST | {
        "a2": (OWN, (2, 0), None),
        "bp": (OTHER, (1, 0), None), "bm": (OTHER, (-1, 0), None), "b2": (OTHER, (2, 0), None),
    },
    {"az": ("bp", "bm", "b2")},
    [("az",), ("ap",), ("am",), ("a2",), ("bp",), ("bm",), ("b2",)],
)


TASKS = (
    ((0, 0), (0, 0), 0, (0, 0)),
    ((0, 1), (0, 0), 0, (0, 1)),
    ((1, 0), (0, 0), 0, (1, 0)),
    ((0, 1), (1, 0), 1, (-1, 1)),
    ((-1, 0), (0, 0), 0, (-1, 0)),
    ((0, 1), (-1, 0), -1, (1, 1)),
    ((1, 0), (-1, 0), -1, (2, 0)),
    ((1, 1), (-1, 0), -1, (2, 1)),
)
HOPS = (3, 5, 6, 7)


class Gather:
    def __init__(self, way, view, place, device, send, recv):
        self.plan, self.after, self.order = way
        self.view, self.place, self.device, self.send, self.recv = view, place, device, send, recv
        self.names = list(self.plan)
        self.taken = 0

    def copy(self, name, receiving):
        (d, dz), (step, flip), part = self.plan[name]
        if receiving:
            d, dz = d - step, (dz + flip) % 2
        i = self.names.index(name)
        ref = self.view(self.place(d, dz), part)
        return pltpu.make_async_remote_copy(
            src_ref=ref, dst_ref=ref, send_sem=self.send.at[i], recv_sem=self.recv.at[i],
            device_id=self.device(step, flip), device_id_type=MESH,
        )

    def begin(self):
        for name in self.names:
            if name[0] == "a":
                self.copy(name, False).start()

    def take(self):
        names = self.order[self.taken]
        self.taken += 1
        for name in names:
            self.copy(name, True).wait_recv()
            for nxt in self.after.get(name, ()):
                self.copy(nxt, False).start()
        (d, dz), (step, flip), _ = self.plan[names[0]]
        return (d - step + 1) % 4 - 1, (dz + flip) % 2

    def end(self):
        assert self.taken == len(self.order)
        for name in self.names:
            self.copy(name, False).wait_send()


def kernel(
    x_ref, o_ref, xkept, xin, xb, gp, crecv, own, rsst, rsrecv, hopst, hoprecv, rzst, rzrecv, rzown, ga, gc, pc, acc, uo, urecv,
    ts, tr, gs, gr, hs, hr, ps, pr, ks, xs, xr, cs, cr, rss, rsr, hs2, hr2, zs, zr, shs, shr, pss, psr, us, ur,
):
    w = Where()
    c = w.c
    rows, width = x_ref.shape
    half, full, quarter = rows // 2, 2 * width, width // 4
    mate = w.device(dc=1)

    peers = [dict(dc=1), dict(dy=1), dict(dy=-1), dict(dy=2), dict(dzl=1), dict(dx=1), dict(dx=-1), dict(dx=2), dict(dzh=1)]
    barrier = pltpu.get_barrier_semaphore()
    for peer in peers:
        pl.semaphore_signal(barrier, inc=1, device_id=w.device(**peer), device_id_type=MESH)
    pl.semaphore_wait(barrier, len(peers))

    def remote(src, dst, send, recv, device):
        return pltpu.make_async_remote_copy(
            src_ref=src, dst_ref=dst, send_sem=send, recv_sem=recv, device_id=device, device_id_type=MESH
        )

    swap = remote(x_ref.at[pl.ds((1 - c) * half, half), :], xin, xs, xr, mate)
    swap.start()
    keep = pltpu.make_async_copy(x_ref.at[pl.ds(c * half, half), :], xkept, ks)
    keep.start()
    mine = w.y * 2 + w.zl
    keep.wait()
    swap.wait_recv()
    kept, got = xkept[...], xin[...]
    xb[mine] = jnp.concatenate([jnp.where(c == 0, kept, got), jnp.where(c == 0, got, kept)], axis=1)

    def tdevice(step, flip):
        return w.device(dy=step, dzl=flip)

    def fdevice(step, flip):
        return w.device(dx=step, dzh=flip)

    def slot_of(rel):
        y, zl = w.tplace(*rel)
        return y * 2 + zl

    part_rows = (half // 32 + 1) * 16

    def xview(place, part):
        at, size = ((0, half), (0, part_rows), (part_rows, half - part_rows))[0 if part is None else part + 1]
        return xb.at[place[0] * 2 + place[1], pl.ds(at, size), :]

    gx = Gather(TWICE, xview, w.tplace, tdevice, ts, tr)
    gx.begin()
    other_rows = pl.ds((1 - c) * width, width)
    kept_rows = pl.ds(c * width, width)
    kept_quarter = pl.ds(c * width + w.x * quarter, quarter)
    done = []

    def gram(task):
        buf = len(done) % GP
        done.append(task)
        j, k = TASKS[task][:2]
        gp[buf] = lax.dot_general(
            xb[slot_of(j)], xb[slot_of(k)], (((0,), (0,)), ((), ())), preferred_element_type=F32
        )
        core_copy(task).start()

    def core_copy(task):
        buf = done.index(task) % GP
        return remote(gp.at[buf, other_rows, :], crecv.at[task], cs.at[task], cr.at[task], mate)

    def x_copy(task, d):
        to = (w.x + d) % 4
        return remote(
            rsst.at[task, pl.ds(to * quarter, quarter), :], rsrecv.at[d - 1, task],
            rss.at[task, d - 1], rsr.at[d - 1, task], w.device(dx=d),
        )

    def hop_copy(task):
        i = HOPS.index(task)
        return remote(hopst.at[i], hoprecv.at[i], hs2.at[i], hr2.at[i], w.device(dy=TASKS[task][2]))

    def z_copy(i):
        return remote(rzst.at[i], rzrecv.at[i], zs.at[i], zr.at[i], w.device(dzh=1))

    def scatter(task):
        buf = done.index(task) % GP
        core_copy(task).wait_recv()
        core_copy(task).wait_send()
        own[task] = gp[buf, kept_quarter, :] + crecv[task, pl.ds(w.x * quarter, quarter), :]
        rsst[task] = (gp[buf, kept_rows, :] + crecv[task]).astype(BF16)
        for d in (1, 2, 3):
            x_copy(task, d).start()

    def summed(task):
        for d in (1, 2, 3):
            x_copy(task, d).wait_recv()
        total = own[task] + sum(rsrecv[d, task].astype(F32) for d in range(3))
        if task in HOPS:
            hopst[HOPS.index(task)] = total.astype(BF16)
            hop_copy(task).start()
        else:
            placed(task, total)

    def hopped(task):
        hop_copy(task).wait_recv()
        placed(task, hoprecv[HOPS.index(task)].astype(F32))

    def placed(task, total):
        i, dz = TASKS[task][3]
        i = i % 4
        there = (w.zl + dz) % 2 != w.zh

        @pl.when(there)
        def _():
            rzst[i] = total.astype(BF16)
            z_copy(i).start()

        @pl.when(jnp.logical_not(there))
        def _():
            rzown[i] = total

    part = (quarter // 32 + 1) * 16
    parts = ((0, quarter), (0, part), (part, quarter - part))

    def chunk(i, way_f, way_t):
        def cview(place, half_of):
            at, size = parts[0 if half_of is None else half_of + 1]
            return gc.at[(w.y + i) % 4, place[1], pl.ds(c * width + place[0] * quarter + at, size), :]

        def aview(place, half_of):
            at, size = parts[0 if half_of is None else half_of + 1]
            return ga.at[place[0] * 2 + place[1], (place[0] + i) % 4, pl.ds(at, size), :]

        return (
            Gather(way_f, cview, w.fplace, fdevice, gs.at[i], gr.at[i]),
            Gather(way_t, aview, w.tplace, tdevice, hs.at[i], hr.at[i]),
        )

    chunks = {0: chunk(0, ONCE, ONCE), 1: chunk(1, ONCE, ONCE), 3: chunk(3, ONCE, ONCE), 2: chunk(2, DIRECT, DIRECT)}

    def share(i, place, other=False):
        x, zh = place
        core = 1 - c if other else c
        ref = gc.at[(w.y + i) % 4, zh, pl.ds(core * width + x * quarter, quarter), :]
        return remote(ref, ref, shs.at[i, x * 2 + zh], shr.at[i, x * 2 + zh], mate)

    def ready(i):
        z_copy(i).wait_recv()
        block = (rzown[i] + rzrecv[i].astype(F32)).astype(BF16)
        at = (w.y + i) % 4
        ga[mine, at] = block
        gc[at, w.zh, kept_quarter, :] = block
        for g in chunks[i]:
            g.begin()
        share(i, w.fplace(0, 0)).start()

    def take_f(i, count):
        for _ in range(count):
            share(i, w.fplace(*chunks[i][0].take())).start()

    def take_t(i, count):
        for _ in range(count):
            chunks[i][1].take()

    gram(0)
    scatter(0)
    summed(0)
    for _ in range(3):
        gx.take()
    gram(1)
    gram(2)
    scatter(1)
    gram(5)
    scatter(2)
    gram(4)
    scatter(5)
    gram(3)
    scatter(4)
    gram(6)
    scatter(3)
    scatter(6)
    summed(1)
    ready(0)
    summed(2)
    summed(5)
    summed(4)
    for _ in range(3):
        gx.take()
    gram(7)
    scatter(7)
    hopped(5)
    ready(1)
    summed(3)
    take_f(0, 3)
    take_t(0, 3)
    summed(6)
    hopped(3)
    ready(3)
    take_f(0, 2)
    take_t(0, 2)
    take_f(1, 3)
    take_t(1, 3)
    gx.take()
    hopped(6)
    summed(7)
    take_f(0, 2)
    take_t(0, 2)
    take_f(1, 2)
    take_t(1, 2)
    hopped(7)
    ready(2)
    take_f(3, 3)
    take_t(3, 3)
    take_f(1, 2)
    take_t(1, 2)
    take_f(3, 2)
    take_t(3, 2)
    take_f(2, 4)
    take_t(2, 4)
    take_f(3, 2)
    take_t(3, 2)
    take_f(2, 3)
    take_t(2, 3)
    for i in range(4):
        for j in range(8):
            share(i, (j // 2, j % 2), True).wait_recv()

    total = jnp.dot(
        jnp.concatenate([ga[j].reshape(width, full) for j in range(8)], axis=1),
        gc[...].reshape(8 * full, full), preferred_element_type=F32,
    )
    value = (C * total + B * ga[mine].reshape(width, full).astype(F32)).astype(BF16)
    for i in range(4):
        pc[i, w.zh, kept_quarter, :] = value[i * quarter:(i + 1) * quarter]

    def pview(place, half_of):
        which = pl.ds(0, 4) if half_of is None else pl.ds(2 * half_of, 2)
        return pc.at[which, place[1], pl.ds(c * width + place[0] * quarter, quarter), :]

    def share_p(place, other=False):
        x, zh = place
        core = 1 - c if other else c
        ref = pc.at[:, zh, pl.ds(core * width + x * quarter, quarter), :]
        return remote(ref, ref, pss.at[x * 2 + zh], psr.at[x * 2 + zh], mate)

    gpc = Gather(TWICE, pview, w.fplace, fdevice, ps, pr)
    gpc.begin()
    share_p(w.fplace(0, 0)).start()
    tile_rows = half // 5

    def product(zh, first):
        for x in range(4):
            share_p((x, zh), True).wait_recv()

        left = jnp.concatenate([xb[j * 2 + zh] for j in range(4)], axis=1)
        for at in range(0, full, 256):
            cols = pl.ds(at, min(256, full - at))
            right = jnp.concatenate([pc[j, zh, :, cols] for j in range(4)], axis=0)
            start = A * xb[mine, :, cols].astype(F32) if first else acc[:, cols]
            acc[:, cols] = start + jnp.dot(left, right, preferred_element_type=F32)

    for i in range(7):
        if i == 6:
            product(w.zh, True)
        share_p(w.fplace(*gpc.take())).start()
    product(1 - w.zh, False)

    back = remote(uo, urecv, us, ur, mate)

    def split(i, _):
        at = pl.ds(pl.multiple_of(i * tile_rows, tile_rows), tile_rows)
        value = (FACTOR * acc[at, :]).astype(BF16)
        left, right = value[:, :width], value[:, width:]
        first = c == 0
        o_ref[pl.ds(pl.multiple_of(c * half + i * tile_rows, 16), tile_rows), :] = jnp.where(first, left, right)
        uo[at, :] = jnp.where(first, right, left)
        return 0

    lax.fori_loop(0, 5, split, 0)
    back.start()

    swap.wait_send()
    for g in [gx, gpc] + [g for pair in chunks.values() for g in pair]:
        g.end()
    for step in range(8):
        for d in (1, 2, 3):
            x_copy(step, d).wait_send()
    for task in HOPS:
        hop_copy(task).wait_send()
    for i in range(4):
        z_copy(i).wait_send()
    for j in range(8):
        share_p((j // 2, j % 2)).wait_send()
        for i in range(4):
            share(i, (j // 2, j % 2)).wait_send()
    back.wait()
    o_ref[pl.ds((1 - c) * half, half), :] = urecv[...]


def shards(iterate):
    rows, width = iterate.shape
    half, full, quarter = rows // 2, 2 * width, width // 4
    dma = pltpu.SemaphoreType.DMA
    vmem = pltpu.VMEM
    return pl.pallas_call(
        kernel,
        out_shape=jax.ShapeDtypeStruct((rows, width), BF16),
        in_specs=[pl.BlockSpec(memory_space=pl.ANY)],
        out_specs=pl.BlockSpec(memory_space=pltpu.VMEM),
        scratch_shapes=[
            vmem((half, width), BF16),
            vmem((half, width), BF16),
            vmem((8, half, full), BF16),
            vmem((GP, full, full), F32),
            vmem((8, width, full), F32),
            vmem((8, quarter, full), F32),
            vmem((8, width, full), BF16),
            vmem((3, 8, quarter, full), BF16),
            vmem((4, quarter, full), BF16),
            vmem((4, quarter, full), BF16),
            vmem((4, quarter, full), BF16),
            vmem((4, quarter, full), BF16),
            vmem((4, quarter, full), F32),
            vmem((8, 4, quarter, full), BF16),
            vmem((4, 2, full, full), BF16),
            vmem((4, 2, full, full), BF16),
            vmem((half, full), F32),
            vmem((half, width), BF16),
            vmem((half, width), BF16),
            dma((8,)), dma((8,)), dma((4, 9)), dma((4, 9)), dma((4, 9)), dma((4, 9)), dma((8,)), dma((8,)),
            dma, dma, dma, dma((8,)), dma((8,)), dma((8, 3)), dma((3, 8)), dma((4,)), dma((4,)), dma((4,)), dma((4,)),
            dma((4, 8)), dma((4, 8)), dma((8,)), dma((8,)), dma, dma,
        ],
        compiler_params=pltpu.CompilerParams(
            collective_id=0, has_side_effects=True, vmem_limit_bytes=60 * 2**20
        ),
        cost_estimate=pl.CostEstimate(flops=6 * rows * width * 16 * width, bytes_accessed=4 * rows * width, transcendentals=0),
        name="newton_schulz",
    )(iterate)


def solution(mesh):
    return jax.shard_map(
        shards, mesh=mesh, in_specs=(P("fsdp", "tensor"),), out_specs=P("fsdp", "tensor"), check_vma=False
    )
```

```python
import functools

import jax
import jax.numpy as jnp
from jax import lax
from jax.experimental import pallas as pl
from jax.experimental.pallas import tpu as pltpu
from jax.sharding import PartitionSpec as P

MESH = pl.DeviceIdType.MESH
BF16, F32 = jnp.bfloat16, jnp.float32
ROWS = 12800
FACTOR = 0.2 * ROWS**0.5
A, B, C = 3.4445, -4.775, 2.0315
GP = 4


class Where:
    def __init__(self):
        f, t = lax.axis_index("fsdp"), lax.axis_index("tensor")
        self.zh, self.x = f // 4, f % 4
        self.y, self.zl, self.c = t // 4, (t // 2) % 2, t % 2

    def device(self, dx=0, dzh=0, dy=0, dzl=0, dc=0):
        x, y = (self.x + dx) % 4, (self.y + dy) % 4
        zh, zl, c = (self.zh + dzh) % 2, (self.zl + dzl) % 2, (self.c + dc) % 2
        return (zh * 4 + x, y * 4 + zl * 2 + c)

    def tplace(self, d, dz):
        return (self.y + d) % 4, (self.zl + dz) % 2

    def fplace(self, d, dz):
        return (self.x + d) % 4, (self.zh + dz) % 2


OWN, MINUS, PLUS, OTHER = (0, 0), (-1, 0), (1, 0), (0, 1)
FIRST = {"az": (OWN, (0, 1), None), "ap": (OWN, (1, 0), None), "am": (OWN, (-1, 0), None)}
TWICE = (
    FIRST | {
        "bm": (PLUS, (-1, 0), None), "bz": (PLUS, (0, 1), None), "bp": (OTHER, (1, 0), None),
        "cp": ((-1, 1), (1, 0), 0), "cm": ((1, 1), (-1, 0), 1),
    },
    {"am": ("bm", "bz"), "az": ("bp",), "bp": ("cp",), "bz": ("cm",)},
    [("az",), ("am",), ("ap",), ("bp",), ("bz",), ("bm",), ("cp", "cm")],
)
ONCE = (
    FIRST | {
        "bp": (OTHER, (1, 0), None), "bm": (OTHER, (-1, 0), None), "cp": (MINUS, (1, 0), 0), "cm": (PLUS, (-1, 0), 1),
        "dp": ((-1, 1), (1, 0), 0), "dm": ((1, 1), (-1, 0), 1),
    },
    {"az": ("bp", "bm"), "ap": ("cp",), "am": ("cm",), "bp": ("dp",), "bm": ("dm",)},
    [("az",), ("ap",), ("am",), ("bp",), ("bm",), ("cp", "cm"), ("dp", "dm")],
)
HELD = (
    FIRST | {
        "bm": (OTHER, (-1, 0), 0), "bz": (PLUS, (0, 1), 1), "bp": (OTHER, (1, 0), None), "cp": (MINUS, (1, 0), 0),
        "cm": (PLUS, (-1, 0), 1), "dp": ((-1, 1), (1, 0), 0), "dm": ((1, 1), (-1, 0), 1),
    },
    {"az": ("bm", "bp"), "am": ("bz",)},
    [("az",), ("am",), ("ap",), ("bm", "bz"), ("bp",), ("cp", "cm"), ("dp", "dm")],
)
DIRECT = (
    FIRST | {
        "a2": (OWN, (2, 0), None),
        "bp": (OTHER, (1, 0), None), "bm": (OTHER, (-1, 0), None), "b2": (OTHER, (2, 0), None),
    },
    {"az": ("bp", "bm", "b2")},
    [("az",), ("ap",), ("am",), ("a2",), ("bp",), ("bm",), ("b2",)],
)


TASKS = (
    ((0, 0), (0, 0), 0, (0, 0)),
    ((0, 1), (0, 0), 0, (0, 1)),
    ((1, 0), (0, 0), 0, (1, 0)),
    ((0, 1), (1, 0), 1, (-1, 1)),
    ((-1, 0), (0, 0), 0, (-1, 0)),
    ((0, 1), (-1, 0), -1, (1, 1)),
    ((1, 0), (-1, 0), -1, (2, 0)),
    ((1, 1), (-1, 0), -1, (2, 1)),
)
HOPS = (3, 5, 6, 7)


class Gather:
    def __init__(self, way, view, place, device, send, recv):
        self.plan, self.after, self.order = way
        self.view, self.place, self.device, self.send, self.recv = view, place, device, send, recv
        self.names = list(self.plan)
        self.taken = 0

    def copy(self, name, receiving):
        (d, dz), (step, flip), part = self.plan[name]
        if receiving:
            d, dz = d - step, (dz + flip) % 2
        i = self.names.index(name)
        ref = self.view(self.place(d, dz), part)
        return pltpu.make_async_remote_copy(
            src_ref=ref, dst_ref=ref, send_sem=self.send.at[i], recv_sem=self.recv.at[i],
            device_id=self.device(step, flip), device_id_type=MESH,
        )

    def begin(self):
        for name in self.names:
            if name[0] == "a":
                self.copy(name, False).start()

    def take(self):
        names = self.order[self.taken]
        self.taken += 1
        for name in names:
            self.copy(name, True).wait_recv()
            for nxt in self.after.get(name, ()):
                self.copy(nxt, False).start()
        (d, dz), (step, flip), _ = self.plan[names[0]]
        return (d - step + 1) % 4 - 1, (dz + flip) % 2

    def end(self):
        assert self.taken == len(self.order)
        for name in self.names:
            self.copy(name, False).wait_send()


def kernel(
    x_ref, o_ref, xkept, xin, xb, gp, crecv, own, rsst, rlrecv, rsrecv, hopst, hoprecv, rzst, rzrecv, rzown, ga, gc, pc, acc, uo, urecv,
    ts, tr, gs, gr, hs, hr, ps, pr, ks, xs, xr, cs, cr, rss, rsr, hs2, hr2, zs, zr, shs, shr, pss, psr, us, ur,
):
    w = Where()
    c = w.c
    rows, width = x_ref.shape
    half, full, quarter = rows // 2, 2 * width, width // 4
    mate = w.device(dc=1)

    peers = [dict(dc=1), dict(dy=1), dict(dy=-1), dict(dy=2), dict(dzl=1), dict(dx=1), dict(dx=-1), dict(dx=2), dict(dzh=1)]
    barrier = pltpu.get_barrier_semaphore()
    for peer in peers:
        pl.semaphore_signal(barrier, inc=1, device_id=w.device(**peer), device_id_type=MESH)
    pl.semaphore_wait(barrier, len(peers))

    def remote(src, dst, send, recv, device):
        return pltpu.make_async_remote_copy(
            src_ref=src, dst_ref=dst, send_sem=send, recv_sem=recv, device_id=device, device_id_type=MESH
        )

    swap = remote(x_ref.at[pl.ds((1 - c) * half, half), :], xin, xs, xr, mate)
    swap.start()
    keep = pltpu.make_async_copy(x_ref.at[pl.ds(c * half, half), :], xkept, ks)
    keep.start()
    mine = w.y * 2 + w.zl
    keep.wait()
    swap.wait_recv()
    kept, got = xkept[...], xin[...]
    xb[mine] = jnp.concatenate([jnp.where(c == 0, kept, got), jnp.where(c == 0, got, kept)], axis=1)

    def tdevice(step, flip):
        return w.device(dy=step, dzl=flip)

    def fdevice(step, flip):
        return w.device(dx=step, dzh=flip)

    def slot_of(rel):
        y, zl = w.tplace(*rel)
        return y * 2 + zl

    part_rows = (half // 32 + 1) * 16

    def xview(place, part):
        at, size = ((0, half), (0, part_rows), (part_rows, half - part_rows))[0 if part is None else part + 1]
        return xb.at[place[0] * 2 + place[1], pl.ds(at, size), :]

    gx = Gather(HELD, xview, w.tplace, tdevice, ts, tr)
    gx.begin()
    other_rows = pl.ds((1 - c) * width, width)
    kept_rows = pl.ds(c * width, width)
    kept_quarter = pl.ds(c * width + w.x * quarter, quarter)
    done = []

    def gram(task):
        buf = len(done) % GP
        done.append(task)
        j, k = TASKS[task][:2]
        gp[buf] = lax.dot_general(
            xb[slot_of(j)], xb[slot_of(k)], (((0,), (0,)), ((), ())), preferred_element_type=F32
        )
        core_copy(task).start()

    def core_copy(task):
        buf = done.index(task) % GP
        return remote(gp.at[buf, other_rows, :], crecv.at[task], cs.at[task], cr.at[task], mate)

    cut = (quarter // 32 + 1) * 16

    def relay_copy(task, way):
        at, size = ((0, cut), (cut, quarter - cut))[way]
        return remote(
            rsst.at[task, pl.ds((w.x + 2) % 4 * quarter + at, size), :], rlrecv.at[task, pl.ds(at, size), :],
            rss.at[task, way], rsr.at[task, way], w.device(dx=1 - 2 * way),
        )

    def x_copy(task, way):
        return remote(
            rsst.at[task, pl.ds((w.x + 1 - 2 * way) % 4 * quarter, quarter), :], rsrecv.at[way, task],
            rss.at[task, 2 + way], rsr.at[task, 2 + way], w.device(dx=1 - 2 * way),
        )

    def hop_copy(task):
        i = HOPS.index(task)
        return remote(hopst.at[i], hoprecv.at[i], hs2.at[i], hr2.at[i], w.device(dy=TASKS[task][2]))

    def z_copy(i):
        return remote(rzst.at[i], rzrecv.at[i], zs.at[i], zr.at[i], w.device(dzh=1))

    def scatter(task):
        buf = done.index(task) % GP
        core_copy(task).wait_recv()
        core_copy(task).wait_send()
        own[task] = gp[buf, kept_quarter, :] + crecv[task, pl.ds(w.x * quarter, quarter), :]
        rsst[task] = (gp[buf, kept_rows, :] + crecv[task]).astype(BF16)
        for way in (0, 1):
            relay_copy(task, way).start()

    def relayed(task):
        for way, (at, size) in enumerate(((0, cut), (cut, quarter - cut))):
            relay_copy(task, way).wait_recv()
            rows = pl.ds((w.x + 1 - 2 * way) % 4 * quarter + at, size)
            rsst[task, rows, :] = (
                rsst[task, rows, :].astype(F32) + rlrecv[task, pl.ds(at, size), :].astype(F32)
            ).astype(BF16)
            x_copy(task, way).start()

    def summed(task):
        for way in (0, 1):
            x_copy(task, way).wait_recv()
        total = own[task] + rsrecv[0, task].astype(F32) + rsrecv[1, task].astype(F32)
        if task in HOPS:
            hopst[HOPS.index(task)] = total.astype(BF16)
            hop_copy(task).start()
        else:
            placed(task, total)

    def hopped(task):
        hop_copy(task).wait_recv()
        placed(task, hoprecv[HOPS.index(task)].astype(F32))

    def placed(task, total):
        i, dz = TASKS[task][3]
        i = i % 4
        there = (w.zl + dz) % 2 != w.zh

        @pl.when(there)
        def _():
            rzst[i] = total.astype(BF16)
            z_copy(i).start()

        @pl.when(jnp.logical_not(there))
        def _():
            rzown[i] = total

    part = (quarter // 32 + 1) * 16
    parts = ((0, quarter), (0, part), (part, quarter - part))

    def chunk(i, way_f, way_t):
        def cview(place, half_of):
            at, size = parts[0 if half_of is None else half_of + 1]
            return gc.at[(w.y + i) % 4, place[1], pl.ds(c * width + place[0] * quarter + at, size), :]

        def aview(place, half_of):
            at, size = parts[0 if half_of is None else half_of + 1]
            return ga.at[place[0] * 2 + place[1], (place[0] + i) % 4, pl.ds(at, size), :]

        return (
            Gather(way_f, cview, w.fplace, fdevice, gs.at[i], gr.at[i]),
            Gather(way_t, aview, w.tplace, tdevice, hs.at[i], hr.at[i]),
        )

    chunks = {0: chunk(0, ONCE, ONCE), 1: chunk(1, ONCE, ONCE), 3: chunk(3, ONCE, ONCE), 2: chunk(2, DIRECT, DIRECT)}

    def share(i, place, other=False):
        x, zh = place
        core = 1 - c if other else c
        ref = gc.at[(w.y + i) % 4, zh, pl.ds(core * width + x * quarter, quarter), :]
        return remote(ref, ref, shs.at[i, x * 2 + zh], shr.at[i, x * 2 + zh], mate)

    def ready(i):
        z_copy(i).wait_recv()
        block = (rzown[i] + rzrecv[i].astype(F32)).astype(BF16)
        at = (w.y + i) % 4
        ga[mine, at] = block
        gc[at, w.zh, kept_quarter, :] = block
        for g in chunks[i]:
            g.begin()
        share(i, w.fplace(0, 0)).start()

    def take_f(i, count):
        for _ in range(count):
            share(i, w.fplace(*chunks[i][0].take())).start()

    def take_t(i, count):
        for _ in range(count):
            chunks[i][1].take()

    gram(0)
    scatter(0)
    relayed(0)
    summed(0)
    for _ in range(3):
        gx.take()
    gram(1)
    gram(2)
    scatter(1)
    gram(5)
    scatter(2)
    gram(4)
    relayed(1)
    scatter(5)
    gram(3)
    relayed(2)
    scatter(4)
    gram(6)
    relayed(5)
    scatter(3)
    relayed(4)
    scatter(6)
    relayed(3)
    for _ in range(1):
        gx.take()
    gram(7)
    summed(1)
    ready(0)
    relayed(6)
    scatter(7)
    summed(2)
    summed(5)
    take_f(0, 1)
    take_t(0, 1)
    summed(4)
    relayed(7)
    hopped(5)
    ready(1)
    take_f(0, 2)
    take_t(0, 2)
    summed(3)
    summed(6)
    hopped(3)
    take_f(1, 1)
    take_t(1, 1)
    ready(3)
    summed(7)
    hopped(6)
    take_f(0, 2)
    take_t(0, 2)
    take_f(1, 2)
    take_t(1, 2)
    take_f(3, 1)
    take_t(3, 1)
    hopped(7)
    ready(2)
    take_f(0, 2)
    take_t(0, 2)
    take_f(1, 2)
    take_t(1, 2)
    take_f(3, 2)
    take_t(3, 2)
    take_f(2, 1)
    take_t(2, 1)
    take_f(2, 2)
    take_t(2, 2)
    take_f(1, 2)
    take_t(1, 2)
    take_f(3, 2)
    take_t(3, 2)
    take_f(2, 2)
    take_t(2, 2)
    take_f(3, 2)
    take_t(3, 2)
    take_f(2, 2)
    take_t(2, 2)
    for _ in range(1):
        gx.take()
    for name in ("cp", "cm", "dp", "dm"):
        gx.copy(name, False).start()
    for i in range(4):
        for j in range(8):
            share(i, (j // 2, j % 2), True).wait_recv()

    columns = [pl.ds(at, min(384, full - at)) for at in range(0, full, 384)]

    def pview(cols):
        def view(place, half_of):
            which = pl.ds(0, 4) if half_of is None else pl.ds(2 * half_of, 2)
            return pc.at[which, place[1], pl.ds(c * width + place[0] * quarter, quarter), cols]

        return view

    def share_p(n, place, other=False):
        x, zh = place
        core = 1 - c if other else c
        ref = pc.at[:, zh, pl.ds(core * width + x * quarter, quarter), columns[n]]
        return remote(ref, ref, pss.at[n, x * 2 + zh], psr.at[n, x * 2 + zh], mate)

    gps = [Gather(TWICE, pview(cols), w.fplace, fdevice, ps.at[n], pr.at[n]) for n, cols in enumerate(columns)]
    for n, cols in enumerate(columns):
        total = jnp.dot(
            jnp.concatenate([ga[j].reshape(width, full) for j in range(8)], axis=1),
            jnp.concatenate([gc[j // 2, j % 2, :, cols] for j in range(8)], axis=0),
            preferred_element_type=F32,
        )
        value = (C * total + B * ga[mine, :, :, cols].reshape(width, cols.size).astype(F32)).astype(BF16)
        for i in range(4):
            pc[i, w.zh, kept_quarter, cols] = value[i * quarter:(i + 1) * quarter]
        gps[n].begin()
        share_p(n, w.fplace(0, 0)).start()

    def take_p(n):
        share_p(n, w.fplace(*gps[n].take())).start()

    def arrived(n, zh):
        for x in range(4):
            share_p(n, (x, zh), True).wait_recv()

    def product(n, zh, first, rows=pl.ds(0, half)):
        cols = columns[n]
        left = jnp.concatenate([xb[j * 2 + zh, rows, :] for j in range(4)], axis=1)
        right = jnp.concatenate([pc[j, zh, :, cols] for j in range(4)], axis=0)
        start = A * xb[mine, rows, cols].astype(F32) if first else acc[rows, cols]
        acc[rows, cols] = start + jnp.dot(left, right, preferred_element_type=F32)

    def back(part):
        rows = pl.ds(part * (half // 2), half // 2)
        return remote(uo.at[rows, :], urecv.at[rows, :], us.at[part], ur.at[part], mate)

    for _ in range(6):
        take_p(0)
        take_p(1)
    gx.take()
    gx.take()
    arrived(0, w.zh)
    product(0, w.zh, True)
    take_p(0)
    arrived(1, w.zh)
    product(1, w.zh, True)
    take_p(1)
    arrived(0, 1 - w.zh)
    product(0, 1 - w.zh, False)
    arrived(1, 1 - w.zh)
    for part in (0, 1):
        rows = pl.ds(part * (half // 2), half // 2)
        product(1, 1 - w.zh, False, rows)
        value = (FACTOR * acc[rows, :]).astype(BF16)
        left, right = value[:, :width], value[:, width:]
        first = c == 0
        uo[rows, :] = jnp.where(first, right, left)
        back(part).start()
        o_ref[pl.ds(pl.multiple_of(c * half + part * (half // 2), 16), half // 2), :] = jnp.where(first, left, right)

    swap.wait_send()
    for g in [gx] + gps + [g for pair in chunks.values() for g in pair]:
        g.end()
    for step in range(8):
        for way in (0, 1):
            relay_copy(step, way).wait_send()
            x_copy(step, way).wait_send()
    for task in HOPS:
        hop_copy(task).wait_send()
    for i in range(4):
        z_copy(i).wait_send()
    for j in range(8):
        for n in (0, 1):
            share_p(n, (j // 2, j % 2)).wait_send()
        for i in range(4):
            share(i, (j // 2, j % 2)).wait_send()
    for part in (0, 1):
        back(part).wait()
    o_ref[pl.ds((1 - c) * half, half), :] = urecv[...]


def shards(iterate):
    rows, width = iterate.shape
    half, full, quarter = rows // 2, 2 * width, width // 4
    dma = pltpu.SemaphoreType.DMA
    vmem = pltpu.VMEM
    return pl.pallas_call(
        kernel,
        out_shape=jax.ShapeDtypeStruct((rows, width), BF16),
        in_specs=[pl.BlockSpec(memory_space=pl.ANY)],
        out_specs=pl.BlockSpec(memory_space=pltpu.VMEM),
        scratch_shapes=[
            vmem((half, width), BF16),
            vmem((half, width), BF16),
            vmem((8, half, full), BF16),
            vmem((GP, full, full), F32),
            vmem((8, width, full), F32),
            vmem((8, quarter, full), F32),
            vmem((8, width, full), BF16),
            vmem((8, quarter, full), BF16),
            vmem((2, 8, quarter, full), BF16),
            vmem((4, quarter, full), BF16),
            vmem((4, quarter, full), BF16),
            vmem((4, quarter, full), BF16),
            vmem((4, quarter, full), BF16),
            vmem((4, quarter, full), F32),
            vmem((8, 4, quarter, full), BF16),
            vmem((4, 2, full, full), BF16),
            vmem((4, 2, full, full), BF16),
            vmem((half, full), F32),
            vmem((half, width), BF16),
            vmem((half, width), BF16),
            dma((10,)), dma((10,)), dma((4, 9)), dma((4, 9)), dma((4, 9)), dma((4, 9)), dma((2, 8)), dma((2, 8)),
            dma, dma, dma, dma((8,)), dma((8,)), dma((8, 4)), dma((8, 4)), dma((4,)), dma((4,)), dma((4,)), dma((4,)),
            dma((4, 8)), dma((4, 8)), dma((2, 8)), dma((2, 8)), dma((2,)), dma((2,)),
        ],
        compiler_params=pltpu.CompilerParams(
            collective_id=0, has_side_effects=True, vmem_limit_bytes=60 * 2**20
        ),
        cost_estimate=pl.CostEstimate(flops=6 * rows * width * 16 * width, bytes_accessed=4 * rows * width, transcendentals=0),
        name="newton_schulz",
    )(iterate)


def solution(mesh):
    return jax.shard_map(
        shards, mesh=mesh, in_specs=(P("fsdp", "tensor"),), out_specs=P("fsdp", "tensor"), check_vma=False
    )
```

```python
import functools

import jax
import jax.numpy as jnp
from jax import lax
from jax.experimental import pallas as pl
from jax.experimental.pallas import tpu as pltpu
from jax.sharding import PartitionSpec as P

MESH = pl.DeviceIdType.MESH
BF16, F32 = jnp.bfloat16, jnp.float32
ROWS = 12800
FACTOR = 0.2 * ROWS**0.5
A, B, C = 3.4445, -4.775, 2.0315
GP = 4


class Where:
    def __init__(self):
        f, t = lax.axis_index("fsdp"), lax.axis_index("tensor")
        self.zh, self.x = f // 4, f % 4
        self.y, self.zl, self.c = t // 4, (t // 2) % 2, t % 2

    def device(self, dx=0, dzh=0, dy=0, dzl=0, dc=0):
        x, y = (self.x + dx) % 4, (self.y + dy) % 4
        zh, zl, c = (self.zh + dzh) % 2, (self.zl + dzl) % 2, (self.c + dc) % 2
        return (zh * 4 + x, y * 4 + zl * 2 + c)

    def tplace(self, d, dz):
        return (self.y + d) % 4, (self.zl + dz) % 2

    def fplace(self, d, dz):
        return (self.x + d) % 4, (self.zh + dz) % 2


OWN, MINUS, PLUS, OTHER = (0, 0), (-1, 0), (1, 0), (0, 1)
FIRST = {"az": (OWN, (0, 1), None), "ap": (OWN, (1, 0), None), "am": (OWN, (-1, 0), None)}
TWICE = (
    FIRST | {
        "bm": (PLUS, (-1, 0), None), "bz": (PLUS, (0, 1), None), "bp": (OTHER, (1, 0), None),
        "cp": ((-1, 1), (1, 0), 0), "cm": ((1, 1), (-1, 0), 1),
    },
    {"am": ("bm", "bz"), "az": ("bp",), "bp": ("cp",), "bz": ("cm",)},
    [("az",), ("am",), ("ap",), ("bp",), ("bz",), ("bm",), ("cp", "cm")],
)
ONCE = (
    FIRST | {
        "bp": (OTHER, (1, 0), None), "bm": (OTHER, (-1, 0), None), "cp": (MINUS, (1, 0), 0), "cm": (PLUS, (-1, 0), 1),
        "dp": ((-1, 1), (1, 0), 0), "dm": ((1, 1), (-1, 0), 1),
    },
    {"az": ("bp", "bm"), "ap": ("cp",), "am": ("cm",), "bp": ("dp",), "bm": ("dm",)},
    [("az",), ("ap",), ("am",), ("bp",), ("bm",), ("cp", "cm"), ("dp", "dm")],
)
HELD = (
    FIRST | {
        "bm": (OTHER, (-1, 0), 0), "bz": (PLUS, (0, 1), 1), "bp": (OTHER, (1, 0), None), "cp": (MINUS, (1, 0), 0),
        "cm": (PLUS, (-1, 0), 1), "dp": ((-1, 1), (1, 0), 0), "dm": ((1, 1), (-1, 0), 1),
    },
    {"az": ("bm", "bp"), "am": ("bz",)},
    [("az",), ("am",), ("ap",), ("bm", "bz"), ("bp",), ("cp", "cm"), ("dp", "dm")],
)
DIRECT = (
    FIRST | {
        "a2": (OWN, (2, 0), None),
        "bp": (OTHER, (1, 0), None), "bm": (OTHER, (-1, 0), None), "b2": (OTHER, (2, 0), None),
    },
    {"az": ("bp", "bm", "b2")},
    [("az",), ("ap",), ("am",), ("a2",), ("bp",), ("bm",), ("b2",)],
)


TASKS = (
    ((0, 0), (0, 0), 0, (0, 0)),
    ((0, 1), (0, 0), 0, (0, 1)),
    ((1, 0), (0, 0), 0, (1, 0)),
    ((0, 1), (1, 0), 1, (-1, 1)),
    ((-1, 0), (0, 0), 0, (-1, 0)),
    ((0, 1), (-1, 0), -1, (1, 1)),
    ((1, 0), (-1, 0), -1, (2, 0)),
    ((1, 1), (-1, 0), -1, (2, 1)),
)
HOPS = (3, 5, 6, 7)
ORDER = (0, 1, 3, 2)
STRAIGHT = (0, 1, 2, 3, 4, 5, 6, 7)


class Gather:
    def __init__(self, way, view, place, device, send, recv):
        self.plan, self.after, self.order = way
        self.view, self.place, self.device, self.send, self.recv = view, place, device, send, recv
        self.names = list(self.plan)
        self.taken = 0

    def copy(self, name, receiving):
        (d, dz), (step, flip), part = self.plan[name]
        if receiving:
            d, dz = d - step, (dz + flip) % 2
        i = self.names.index(name)
        ref = self.view(self.place(d, dz), part)
        return pltpu.make_async_remote_copy(
            src_ref=ref, dst_ref=ref, send_sem=self.send.at[i], recv_sem=self.recv.at[i],
            device_id=self.device(step, flip), device_id_type=MESH,
        )

    def begin(self):
        for name in self.names:
            if name[0] == "a":
                self.copy(name, False).start()

    def take(self):
        names = self.order[self.taken]
        self.taken += 1
        for name in names:
            self.copy(name, True).wait_recv()
            for nxt in self.after.get(name, ()):
                self.copy(nxt, False).start()
        (d, dz), (step, flip), _ = self.plan[names[0]]
        return (d - step + 1) % 4 - 1, (dz + flip) % 2

    def end(self):
        assert self.taken == len(self.order)
        for name in self.names:
            self.copy(name, False).wait_send()


def kernel(
    x_ref, o_ref, xkept, xin, xb, gp, crecv, own, rsst, rlrecv, rsrecv, hopst, hoprecv, rzst, rzrecv, rzown, ga, gc, pc, acc, uo, urecv,
    ts, tr, gs, gr, hs, hr, ps, pr, ks, xs, xr, cs, cr, rss, rsr, hs2, hr2, zs, zr, shs, shr, pss, psr, us, ur,
):
    w = Where()
    c = w.c
    rows, width = x_ref.shape
    half, full, quarter = rows // 2, 2 * width, width // 4
    mate = w.device(dc=1)

    peers = [dict(dc=1), dict(dy=1), dict(dy=-1), dict(dy=2), dict(dzl=1), dict(dx=1), dict(dx=-1), dict(dx=2), dict(dzh=1),
             dict(dy=1, dzh=1), dict(dy=-1, dzh=1)]
    barrier = pltpu.get_barrier_semaphore()
    for peer in peers:
        pl.semaphore_signal(barrier, inc=1, device_id=w.device(**peer), device_id_type=MESH)
    pl.semaphore_wait(barrier, len(peers))

    def remote(src, dst, send, recv, device):
        return pltpu.make_async_remote_copy(
            src_ref=src, dst_ref=dst, send_sem=send, recv_sem=recv, device_id=device, device_id_type=MESH
        )

    swap = remote(x_ref.at[pl.ds((1 - c) * half, half), :], xin, xs, xr, mate)
    swap.start()
    keep = pltpu.make_async_copy(x_ref.at[pl.ds(c * half, half), :], xkept, ks)
    keep.start()
    mine = w.y * 2 + w.zl
    keep.wait()
    swap.wait_recv()
    kept, got = xkept[...], xin[...]
    xb[mine] = jnp.concatenate([jnp.where(c == 0, kept, got), jnp.where(c == 0, got, kept)], axis=1)

    def tdevice(step, flip):
        return w.device(dy=step, dzl=flip)

    def fdevice(step, flip):
        return w.device(dx=step, dzh=flip)

    def slot_of(rel):
        y, zl = w.tplace(*rel)
        return y * 2 + zl

    part_rows = (half // 32 + 1) * 16

    def xview(place, part):
        at, size = ((0, half), (0, part_rows), (part_rows, half - part_rows))[0 if part is None else part + 1]
        return xb.at[place[0] * 2 + place[1], pl.ds(at, size), :]

    gx = Gather(HELD, xview, w.tplace, tdevice, ts, tr)
    gx.begin()
    other_rows = pl.ds((1 - c) * width, width)
    kept_rows = pl.ds(c * width, width)
    kept_quarter = pl.ds(c * width + w.x * quarter, quarter)
    done = []

    def gram(task):
        buf = len(done) % GP
        done.append(task)
        j, k = TASKS[task][:2]
        gp[buf] = lax.dot_general(
            xb[slot_of(j)], xb[slot_of(k)], (((0,), (0,)), ((), ())), preferred_element_type=F32
        )
        core_copy(task).start()

    def core_copy(task):
        buf = done.index(task) % GP
        return remote(gp.at[buf, other_rows, :], crecv.at[task], cs.at[task], cr.at[task], mate)

    cut = (quarter // 32 + 1) * 16

    def cuts(task):
        first = cut if task % 2 else quarter - cut
        return (0, first), (first, quarter - first)

    def relay_copy(task, way):
        at, size = cuts(task)[way]
        return remote(
            rsst.at[task, pl.ds((w.x + 2) % 4 * quarter + at, size), :], rlrecv.at[task, pl.ds(at, size), :],
            rss.at[task, way], rsr.at[task, way], w.device(dx=1 - 2 * way),
        )

    def opposite_copy(task):
        return remote(
            rsst.at[task, pl.ds((w.x + 2) % 4 * quarter, quarter), :], rlrecv.at[task],
            rss.at[task, 0], rsr.at[task, 0], w.device(dx=2),
        )

    def x_copy(task, way):
        return remote(
            rsst.at[task, pl.ds((w.x + 1 - 2 * way) % 4 * quarter, quarter), :], rsrecv.at[way, task],
            rss.at[task, 2 + way], rsr.at[task, 2 + way], w.device(dx=1 - 2 * way),
        )

    def hop_copy(task):
        i = HOPS.index(task)
        return remote(hopst.at[i], hoprecv.at[i], hs2.at[i], hr2.at[i], w.device(dy=TASKS[task][2]))

    def z_copy(i, hop=0):
        return remote(rzst.at[i], rzrecv.at[i], zs.at[i], zr.at[i], w.device(dy=hop, dzh=1))

    def leaves(task):
        return (w.zl + TASKS[task][3][1]) % 2 != w.zh

    def scatter(task):
        buf = done.index(task) % GP
        core_copy(task).wait_recv()
        core_copy(task).wait_send()
        own[task] = gp[buf, kept_quarter, :] + crecv[task, pl.ds(w.x * quarter, quarter), :]
        rsst[task] = (gp[buf, kept_rows, :] + crecv[task]).astype(BF16)
        if task in STRAIGHT:
            opposite_copy(task).start()
            for way in (0, 1):
                x_copy(task, way).start()
        else:
            for way in (0, 1):
                relay_copy(task, way).start()

    def relayed(task):
        if task in STRAIGHT:
            return
        for way, (at, size) in enumerate(cuts(task)):
            relay_copy(task, way).wait_recv()
            rows = pl.ds((w.x + 1 - 2 * way) % 4 * quarter + at, size)
            rsst[task, rows, :] = (
                rsst[task, rows, :].astype(F32) + rlrecv[task, pl.ds(at, size), :].astype(F32)
            ).astype(BF16)
            x_copy(task, way).start()

    def summed(task):
        for way in (0, 1):
            x_copy(task, way).wait_recv()
        total = own[task] + rsrecv[0, task].astype(F32) + rsrecv[1, task].astype(F32)
        if task in STRAIGHT:
            opposite_copy(task).wait_recv()
            total += rlrecv[task].astype(F32)
        hop, (i, _) = TASKS[task][2:]
        i = i % 4

        @pl.when(leaves(task))
        def _():
            rzst[i] = total.astype(BF16)
            z_copy(i, hop).start()

        @pl.when(jnp.logical_not(leaves(task)))
        def _():
            if hop:
                hopst[HOPS.index(task)] = total.astype(BF16)
                hop_copy(task).start()
            else:
                rzown[i] = total

    def hopped(task):
        @pl.when(jnp.logical_not(leaves(task)))
        def _():
            hop_copy(task).wait_recv()
            rzown[TASKS[task][3][0] % 4] = hoprecv[HOPS.index(task)].astype(F32)

    def chunk(n, way_f, way_t):
        def which(half_of):
            return pl.ds(2 * n, 2) if half_of is None else pl.ds(2 * n + half_of, 1)

        def cview(place, half_of):
            return gc.at[which(half_of), place[1], pl.ds(c * width + place[0] * quarter, quarter), :]

        def aview(place, half_of):
            return ga.at[place[0] * 2 + place[1], which(half_of)]

        return (
            Gather(way_f, cview, w.fplace, fdevice, gs.at[n], gr.at[n]),
            Gather(way_t, aview, w.tplace, tdevice, hs.at[n], hr.at[n]),
        )

    chunks = (chunk(0, ONCE, TWICE), chunk(1, ONCE, TWICE))

    def share(n, place, other=False):
        x, zh = place
        core = 1 - c if other else c
        ref = gc.at[pl.ds(2 * n, 2), zh, pl.ds(core * width + x * quarter, quarter), :]
        return remote(ref, ref, shs.at[n, x * 2 + zh], shr.at[n, x * 2 + zh], mate)

    def ready(i):
        z_copy(i).wait_recv()
        block = (rzown[i] + rzrecv[i].astype(F32)).astype(BF16)
        at = ORDER.index(i)
        ga[mine, at] = block
        gc[at, w.zh, kept_quarter, :] = block

    def begin(n):
        for g in chunks[n]:
            g.begin()
        share(n, w.fplace(0, 0)).start()

    def take_f(n, count):
        for _ in range(count):
            share(n, w.fplace(*chunks[n][0].take())).start()

    def take_t(n, count):
        for _ in range(count):
            chunks[n][1].take()

    gram(0)
    scatter(0)
    relayed(0)
    summed(0)
    for _ in range(3):
        gx.take()
    gram(1)
    gram(2)
    scatter(1)
    gram(5)
    scatter(2)
    gram(4)
    scatter(5)
    gram(3)
    scatter(4)
    gram(6)
    scatter(3)
    scatter(6)
    for _ in range(1):
        gx.take()
    gram(7)
    scatter(7)
    summed(1)
    summed(2)
    summed(5)
    ready(0)
    hopped(5)
    ready(1)
    begin(0)
    summed(4)
    summed(3)
    summed(6)
    summed(7)
    hopped(3)
    ready(3)
    hopped(6)
    hopped(7)
    ready(2)
    begin(1)
    take_f(0, 3)
    take_t(0, 3)
    take_f(1, 3)
    take_t(1, 3)
    take_f(0, 2)
    take_t(0, 2)
    take_f(1, 2)
    take_t(1, 2)
    take_f(0, 2)
    take_t(0, 2)
    take_f(1, 2)
    take_t(1, 2)
    for _ in range(1):
        gx.take()
    for name in ("cp", "cm", "dp", "dm"):
        gx.copy(name, False).start()
    for n in range(2):
        for j in range(8):
            share(n, (j // 2, j % 2), True).wait_recv()

    columns = [pl.ds(at, min(384, full - at)) for at in range(0, full, 384)]

    def pview(cols):
        def view(place, half_of):
            which = pl.ds(0, 4) if half_of is None else pl.ds(2 * half_of, 2)
            return pc.at[which, place[1], pl.ds(c * width + place[0] * quarter, quarter), cols]

        return view

    def share_p(n, place, other=False):
        x, zh = place
        core = 1 - c if other else c
        ref = pc.at[:, zh, pl.ds(core * width + x * quarter, quarter), columns[n]]
        return remote(ref, ref, pss.at[n, x * 2 + zh], psr.at[n, x * 2 + zh], mate)

    gps = [Gather(TWICE, pview(cols), w.fplace, fdevice, ps.at[n], pr.at[n]) for n, cols in enumerate(columns)]
    def rows_of(at, zl):
        slot = (w.y + ORDER[at]) % 4 * 2 + zl
        return jnp.concatenate([ga[slot, ORDER.index((i - ORDER[at]) % 4)] for i in ORDER], axis=0)

    depth = [(at, zl) for at in range(4) for zl in range(2)]
    for n, cols in enumerate(columns):
        total = jnp.dot(
            jnp.concatenate([rows_of(at, zl) for at, zl in depth], axis=1),
            jnp.concatenate([gc[at, zl, :, cols] for at, zl in depth], axis=0),
            preferred_element_type=F32,
        )
        value = (C * total + B * ga[mine, :, :, cols].reshape(width, cols.size).astype(F32)).astype(BF16)
        for at, i in enumerate(ORDER):
            pc[(w.y + i) % 4, w.zh, kept_quarter, cols] = value[at * quarter:(at + 1) * quarter]
        gps[n].begin()
        share_p(n, w.fplace(0, 0)).start()

    def take_p(n):
        share_p(n, w.fplace(*gps[n].take())).start()

    def arrived(n, zh):
        for x in range(4):
            share_p(n, (x, zh), True).wait_recv()

    def product(n, zh, first, rows=pl.ds(0, half)):
        cols = columns[n]
        left = jnp.concatenate([xb[j * 2 + zh, rows, :] for j in range(4)], axis=1)
        right = jnp.concatenate([pc[j, zh, :, cols] for j in range(4)], axis=0)
        start = A * xb[mine, rows, cols].astype(F32) if first else acc[rows, cols]
        acc[rows, cols] = start + jnp.dot(left, right, preferred_element_type=F32)

    def back(part):
        rows = pl.ds(part * (half // 2), half // 2)
        return remote(uo.at[rows, :], urecv.at[rows, :], us.at[part], ur.at[part], mate)

    for _ in range(6):
        take_p(0)
        take_p(1)
    gx.take()
    gx.take()
    arrived(0, w.zh)
    product(0, w.zh, True)
    take_p(0)
    arrived(1, w.zh)
    product(1, w.zh, True)
    take_p(1)
    arrived(0, 1 - w.zh)
    product(0, 1 - w.zh, False)
    arrived(1, 1 - w.zh)
    for part in (0, 1):
        rows = pl.ds(part * (half // 2), half // 2)
        product(1, 1 - w.zh, False, rows)
        value = (FACTOR * acc[rows, :]).astype(BF16)
        left, right = value[:, :width], value[:, width:]
        first = c == 0
        uo[rows, :] = jnp.where(first, right, left)
        back(part).start()
        o_ref[pl.ds(pl.multiple_of(c * half + part * (half // 2), 16), half // 2), :] = jnp.where(first, left, right)

    swap.wait_send()
    for g in [gx] + gps + [g for pair in chunks for g in pair]:
        g.end()
    for step in range(8):
        if step in STRAIGHT:
            opposite_copy(step).wait_send()
        for way in (0, 1):
            if step not in STRAIGHT:
                relay_copy(step, way).wait_send()
            x_copy(step, way).wait_send()
    for task in HOPS:
        @pl.when(jnp.logical_not(leaves(task)))
        def _(task=task):
            hop_copy(task).wait_send()

    for i in range(4):
        z_copy(i).wait_send()
    for j in range(8):
        for n in (0, 1):
            share_p(n, (j // 2, j % 2)).wait_send()
        for n in range(2):
            share(n, (j // 2, j % 2)).wait_send()
    for part in (0, 1):
        back(part).wait()
    o_ref[pl.ds((1 - c) * half, half), :] = urecv[...]


def shards(iterate):
    rows, width = iterate.shape
    half, full, quarter = rows // 2, 2 * width, width // 4
    dma = pltpu.SemaphoreType.DMA
    vmem = pltpu.VMEM
    return pl.pallas_call(
        kernel,
        out_shape=jax.ShapeDtypeStruct((rows, width), BF16),
        in_specs=[pl.BlockSpec(memory_space=pl.ANY)],
        out_specs=pl.BlockSpec(memory_space=pltpu.VMEM),
        scratch_shapes=[
            vmem((half, width), BF16),
            vmem((half, width), BF16),
            vmem((8, half, full), BF16),
            vmem((GP, full, full), F32),
            vmem((8, width, full), F32),
            vmem((8, quarter, full), F32),
            vmem((8, width, full), BF16),
            vmem((8, quarter, full), BF16),
            vmem((2, 8, quarter, full), BF16),
            vmem((4, quarter, full), BF16),
            vmem((4, quarter, full), BF16),
            vmem((4, quarter, full), BF16),
            vmem((4, quarter, full), BF16),
            vmem((4, quarter, full), F32),
            vmem((8, 4, quarter, full), BF16),
            vmem((4, 2, full, full), BF16),
            vmem((4, 2, full, full), BF16),
            vmem((half, full), F32),
            vmem((half, width), BF16),
            vmem((half, width), BF16),
            dma((10,)), dma((10,)), dma((4, 9)), dma((4, 9)), dma((4, 9)), dma((4, 9)), dma((2, 8)), dma((2, 8)),
            dma, dma, dma, dma((8,)), dma((8,)), dma((8, 4)), dma((8, 4)), dma((4,)), dma((4,)), dma((4,)), dma((4,)),
            dma((4, 8)), dma((4, 8)), dma((2, 8)), dma((2, 8)), dma((2,)), dma((2,)),
        ],
        compiler_params=pltpu.CompilerParams(
            collective_id=0, has_side_effects=True, vmem_limit_bytes=60 * 2**20
        ),
        cost_estimate=pl.CostEstimate(flops=6 * rows * width * 16 * width, bytes_accessed=4 * rows * width, transcendentals=0),
        name="newton_schulz",
    )(iterate)


def solution(mesh):
    return jax.shard_map(
        shards, mesh=mesh, in_specs=(P("fsdp", "tensor"),), out_specs=P("fsdp", "tensor"), check_vma=False
    )
```

```python
import functools

import jax
import jax.numpy as jnp
from jax import lax
from jax.experimental import pallas as pl
from jax.experimental.pallas import tpu as pltpu
from jax.sharding import PartitionSpec as P

MESH = pl.DeviceIdType.MESH
BF16, F32 = jnp.bfloat16, jnp.float32
ROWS = 12800
FACTOR = 0.2 * ROWS**0.5
A, B, C = 3.4445, -4.775, 2.0315
GP = 4


class Where:
    def __init__(self):
        f, t = lax.axis_index("fsdp"), lax.axis_index("tensor")
        self.zh, self.x = f // 4, f % 4
        self.y, self.zl, self.c = t // 4, (t // 2) % 2, t % 2

    def device(self, dx=0, dzh=0, dy=0, dzl=0, dc=0):
        x, y = (self.x + dx) % 4, (self.y + dy) % 4
        zh, zl, c = (self.zh + dzh) % 2, (self.zl + dzl) % 2, (self.c + dc) % 2
        return (zh * 4 + x, y * 4 + zl * 2 + c)

    def tplace(self, d, dz):
        return (self.y + d) % 4, (self.zl + dz) % 2

    def fplace(self, d, dz):
        return (self.x + d) % 4, (self.zh + dz) % 2


OWN, MINUS, PLUS, OTHER = (0, 0), (-1, 0), (1, 0), (0, 1)
FIRST = {"az": (OWN, (0, 1), None), "ap": (OWN, (1, 0), None), "am": (OWN, (-1, 0), None)}
TWICE = (
    FIRST | {
        "bm": (PLUS, (-1, 0), None), "bz": (PLUS, (0, 1), None), "bp": (OTHER, (1, 0), None),
        "cp": ((-1, 1), (1, 0), 0), "cm": ((1, 1), (-1, 0), 1),
    },
    {"am": ("bm", "bz"), "az": ("bp",), "bp": ("cp",), "bz": ("cm",)},
    [("az",), ("am",), ("ap",), ("bp",), ("bz",), ("bm",), ("cp", "cm")],
)
ONCE = (
    FIRST | {
        "bp": (OTHER, (1, 0), None), "bm": (OTHER, (-1, 0), None), "cp": (MINUS, (1, 0), 0), "cm": (PLUS, (-1, 0), 1),
        "dp": ((-1, 1), (1, 0), 0), "dm": ((1, 1), (-1, 0), 1),
    },
    {"az": ("bp", "bm"), "ap": ("cp",), "am": ("cm",), "bp": ("dp",), "bm": ("dm",)},
    [("az",), ("ap",), ("am",), ("bp",), ("bm",), ("cp", "cm"), ("dp", "dm")],
)
HELD = (
    FIRST | {
        "bm": (OTHER, (-1, 0), 0), "bz": (PLUS, (0, 1), 1), "bp": (OTHER, (1, 0), None), "cp": (MINUS, (1, 0), 0),
        "cm": (PLUS, (-1, 0), 1), "dp": ((-1, 1), (1, 0), 0), "dm": ((1, 1), (-1, 0), 1),
    },
    {"az": ("bm", "bp"), "am": ("bz",)},
    [("az",), ("am",), ("ap",), ("bm", "bz"), ("bp",), ("cp", "cm"), ("dp", "dm")],
)
DIRECT = (
    FIRST | {
        "a2": (OWN, (2, 0), None),
        "bp": (OTHER, (1, 0), None), "bm": (OTHER, (-1, 0), None), "b2": (OTHER, (2, 0), None),
    },
    {"az": ("bp", "bm", "b2")},
    [("az",), ("ap",), ("am",), ("a2",), ("bp",), ("bm",), ("b2",)],
)


TASKS = (
    ((0, 0), (0, 0), 0, (0, 0)),
    ((0, 1), (0, 0), 0, (0, 1)),
    ((1, 0), (0, 0), 0, (1, 0)),
    ((0, 1), (1, 0), 1, (-1, 1)),
    ((-1, 0), (0, 0), 0, (-1, 0)),
    ((0, 1), (-1, 0), -1, (1, 1)),
    ((1, 0), (-1, 0), -1, (2, 0)),
    ((1, 1), (-1, 0), -1, (2, 1)),
)
HOPS = (3, 5, 6, 7)
ORDER = (0, 1, 3, 2)
STRAIGHT = (0, 3, 4, 5, 6, 7)


class Gather:
    def __init__(self, way, view, place, device, send, recv):
        self.plan, self.after, self.order = way
        self.view, self.place, self.device, self.send, self.recv = view, place, device, send, recv
        self.names = list(self.plan)
        self.taken = 0

    def copy(self, name, receiving):
        (d, dz), (step, flip), part = self.plan[name]
        if receiving:
            d, dz = d - step, (dz + flip) % 2
        i = self.names.index(name)
        ref = self.view(self.place(d, dz), part)
        return pltpu.make_async_remote_copy(
            src_ref=ref, dst_ref=ref, send_sem=self.send.at[i], recv_sem=self.recv.at[i],
            device_id=self.device(step, flip), device_id_type=MESH,
        )

    def begin(self):
        for name in self.names:
            if name[0] == "a":
                self.copy(name, False).start()

    def take(self):
        names = self.order[self.taken]
        self.taken += 1
        for name in names:
            self.copy(name, True).wait_recv()
            for nxt in self.after.get(name, ()):
                self.copy(nxt, False).start()
        (d, dz), (step, flip), _ = self.plan[names[0]]
        return (d - step + 1) % 4 - 1, (dz + flip) % 2

    def end(self):
        assert self.taken == len(self.order)
        for name in self.names:
            self.copy(name, False).wait_send()


def kernel(
    x_ref, o_ref, xkept, xin, xb, gp, crecv, own, rsst, rlrecv, rsrecv, hopst, hoprecv, rzst, rzrecv, rzown, ga, gc, pc, acc, uo, urecv,
    ts, tr, gs, gr, hs, hr, ps, pr, ks, xs, xr, cs, cr, rss, rsr, hs2, hr2, zs, zr, shs, shr, pss, psr, us, ur,
):
    w = Where()
    c = w.c
    rows, width = x_ref.shape
    half, full, quarter = rows // 2, 2 * width, width // 4
    mate = w.device(dc=1)

    peers = [dict(dc=1), dict(dy=1), dict(dy=-1), dict(dy=2), dict(dzl=1), dict(dx=1), dict(dx=-1), dict(dx=2), dict(dzh=1),
             dict(dy=1, dzh=1), dict(dy=-1, dzh=1)]
    barrier = pltpu.get_barrier_semaphore()
    for peer in peers:
        pl.semaphore_signal(barrier, inc=1, device_id=w.device(**peer), device_id_type=MESH)
    pl.semaphore_wait(barrier, len(peers))

    def remote(src, dst, send, recv, device):
        return pltpu.make_async_remote_copy(
            src_ref=src, dst_ref=dst, send_sem=send, recv_sem=recv, device_id=device, device_id_type=MESH
        )

    swap = remote(x_ref.at[pl.ds((1 - c) * half, half), :], xin, xs, xr, mate)
    swap.start()
    keep = pltpu.make_async_copy(x_ref.at[pl.ds(c * half, half), :], xkept, ks)
    keep.start()
    mine = w.y * 2 + w.zl
    keep.wait()
    swap.wait_recv()
    kept, got = xkept[...], xin[...]
    xb[mine] = jnp.concatenate([jnp.where(c == 0, kept, got), jnp.where(c == 0, got, kept)], axis=1)

    def tdevice(step, flip):
        return w.device(dy=step, dzl=flip)

    def fdevice(step, flip):
        return w.device(dx=step, dzh=flip)

    def slot_of(rel):
        y, zl = w.tplace(*rel)
        return y * 2 + zl

    part_rows = (half // 32 + 1) * 16

    def xview(place, part):
        at, size = ((0, half), (0, part_rows), (part_rows, half - part_rows))[0 if part is None else part + 1]
        return xb.at[place[0] * 2 + place[1], pl.ds(at, size), :]

    gx = Gather(HELD, xview, w.tplace, tdevice, ts, tr)
    gx.begin()
    other_rows = pl.ds((1 - c) * width, width)
    kept_rows = pl.ds(c * width, width)
    kept_quarter = pl.ds(c * width + w.x * quarter, quarter)
    done = []

    def gram(task):
        buf = len(done) % GP
        done.append(task)
        j, k = TASKS[task][:2]
        gp[buf] = lax.dot_general(
            xb[slot_of(j)], xb[slot_of(k)], (((0,), (0,)), ((), ())), preferred_element_type=F32
        )
        core_copy(task).start()

    def core_copy(task):
        buf = done.index(task) % GP
        return remote(gp.at[buf, other_rows, :], crecv.at[task], cs.at[task], cr.at[task], mate)

    cut = (quarter // 32 + 1) * 16

    def cuts(task):
        first = cut if task % 2 else quarter - cut
        return (0, first), (first, quarter - first)

    def relay_copy(task, way):
        at, size = cuts(task)[way]
        return remote(
            rsst.at[task, pl.ds((w.x + 2) % 4 * quarter + at, size), :], rlrecv.at[task, pl.ds(at, size), :],
            rss.at[task, way], rsr.at[task, way], w.device(dx=1 - 2 * way),
        )

    def opposite_copy(task):
        return remote(
            rsst.at[task, pl.ds((w.x + 2) % 4 * quarter, quarter), :], rlrecv.at[task],
            rss.at[task, 0], rsr.at[task, 0], w.device(dx=2),
        )

    def x_copy(task, way):
        return remote(
            rsst.at[task, pl.ds((w.x + 1 - 2 * way) % 4 * quarter, quarter), :], rsrecv.at[way, task],
            rss.at[task, 2 + way], rsr.at[task, 2 + way], w.device(dx=1 - 2 * way),
        )

    def hop_copy(task):
        i = HOPS.index(task)
        return remote(hopst.at[i], hoprecv.at[i], hs2.at[i], hr2.at[i], w.device(dy=TASKS[task][2]))

    def z_copy(i, hop=0):
        return remote(rzst.at[i], rzrecv.at[i], zs.at[i], zr.at[i], w.device(dy=hop, dzh=1))

    def leaves(task):
        return (w.zl + TASKS[task][3][1]) % 2 != w.zh

    def scatter(task):
        buf = done.index(task) % GP
        core_copy(task).wait_recv()
        core_copy(task).wait_send()
        own[task] = gp[buf, kept_quarter, :] + crecv[task, pl.ds(w.x * quarter, quarter), :]
        rsst[task] = (gp[buf, kept_rows, :] + crecv[task]).astype(BF16)
        if task in STRAIGHT:
            opposite_copy(task).start()
            for way in (0, 1):
                x_copy(task, way).start()
        else:
            for way in (0, 1):
                relay_copy(task, way).start()

    def relayed(task):
        if task in STRAIGHT:
            return
        for way, (at, size) in enumerate(cuts(task)):
            relay_copy(task, way).wait_recv()
            rows = pl.ds((w.x + 1 - 2 * way) % 4 * quarter + at, size)
            rsst[task, rows, :] = (
                rsst[task, rows, :].astype(F32) + rlrecv[task, pl.ds(at, size), :].astype(F32)
            ).astype(BF16)
            x_copy(task, way).start()

    def summed(task):
        for way in (0, 1):
            x_copy(task, way).wait_recv()
        total = own[task] + rsrecv[0, task].astype(F32) + rsrecv[1, task].astype(F32)
        if task in STRAIGHT:
            opposite_copy(task).wait_recv()
            total += rlrecv[task].astype(F32)
        hop, (i, _) = TASKS[task][2:]
        i = i % 4

        @pl.when(leaves(task))
        def _():
            rzst[i] = total.astype(BF16)
            z_copy(i, hop).start()

        @pl.when(jnp.logical_not(leaves(task)))
        def _():
            if hop:
                hopst[HOPS.index(task)] = total.astype(BF16)
                hop_copy(task).start()
            else:
                rzown[i] = total

    def hopped(task):
        @pl.when(jnp.logical_not(leaves(task)))
        def _():
            hop_copy(task).wait_recv()
            rzown[TASKS[task][3][0] % 4] = hoprecv[HOPS.index(task)].astype(F32)

    def chunk(n, way_f, way_t):
        def which(half_of):
            return pl.ds(2 * n, 2) if half_of is None else pl.ds(2 * n + half_of, 1)

        def cview(place, half_of):
            return gc.at[which(half_of), place[1], pl.ds(c * width + place[0] * quarter, quarter), :]

        def aview(place, half_of):
            return ga.at[place[0] * 2 + place[1], which(half_of)]

        return (
            Gather(way_f, cview, w.fplace, fdevice, gs.at[n], gr.at[n]),
            Gather(way_t, aview, w.tplace, tdevice, hs.at[n], hr.at[n]),
        )

    chunks = (chunk(0, ONCE, TWICE), chunk(1, ONCE, TWICE))

    def share(n, place, other=False):
        x, zh = place
        core = 1 - c if other else c
        ref = gc.at[pl.ds(2 * n, 2), zh, pl.ds(core * width + x * quarter, quarter), :]
        return remote(ref, ref, shs.at[n, x * 2 + zh], shr.at[n, x * 2 + zh], mate)

    def ready(i):
        z_copy(i).wait_recv()
        block = (rzown[i] + rzrecv[i].astype(F32)).astype(BF16)
        at = ORDER.index(i)
        ga[mine, at] = block
        gc[at, w.zh, kept_quarter, :] = block

    def begin(n):
        for g in chunks[n]:
            g.begin()
        share(n, w.fplace(0, 0)).start()

    def take_f(n, count):
        for _ in range(count):
            share(n, w.fplace(*chunks[n][0].take())).start()

    def take_t(n, count):
        for _ in range(count):
            chunks[n][1].take()

    gram(0)
    scatter(0)
    summed(0)
    for _ in range(3):
        gx.take()
    gram(1)
    gram(2)
    scatter(1)
    gram(5)
    scatter(2)
    gram(4)
    relayed(1)
    scatter(5)
    gram(3)
    relayed(2)
    scatter(4)
    gram(6)
    scatter(3)
    scatter(6)
    for _ in range(1):
        gx.take()
    gram(7)
    scatter(7)
    summed(1)
    summed(2)
    summed(5)
    ready(0)
    hopped(5)
    ready(1)
    begin(0)
    summed(4)
    summed(3)
    summed(6)
    hopped(3)
    ready(3)
    summed(7)
    take_f(0, 3)
    hopped(6)
    hopped(7)
    ready(2)
    begin(1)
    take_t(0, 3)
    take_f(1, 3)
    take_t(1, 3)
    take_f(0, 2)
    take_t(0, 2)
    take_f(1, 2)
    take_t(1, 2)
    take_f(0, 2)
    take_t(0, 2)
    take_f(1, 2)
    take_t(1, 2)
    for _ in range(1):
        gx.take()
    for name in ("cp", "cm", "dp", "dm"):
        gx.copy(name, False).start()
    for n in range(2):
        for j in range(8):
            share(n, (j // 2, j % 2), True).wait_recv()

    columns = [pl.ds(at, min(384, full - at)) for at in range(0, full, 384)]

    def pview(cols):
        def view(place, half_of):
            which = pl.ds(0, 4) if half_of is None else pl.ds(2 * half_of, 2)
            return pc.at[which, place[1], pl.ds(c * width + place[0] * quarter, quarter), cols]

        return view

    def share_p(n, place, other=False):
        x, zh = place
        core = 1 - c if other else c
        ref = pc.at[:, zh, pl.ds(core * width + x * quarter, quarter), columns[n]]
        return remote(ref, ref, pss.at[n, x * 2 + zh], psr.at[n, x * 2 + zh], mate)

    gps = [Gather(TWICE, pview(cols), w.fplace, fdevice, ps.at[n], pr.at[n]) for n, cols in enumerate(columns)]
    def rows_of(at, zl):
        slot = (w.y + ORDER[at]) % 4 * 2 + zl
        return jnp.concatenate([ga[slot, ORDER.index((i - ORDER[at]) % 4)] for i in ORDER], axis=0)

    depth = [(at, zl) for at in range(4) for zl in range(2)]
    for n, cols in enumerate(columns):
        total = jnp.dot(
            jnp.concatenate([rows_of(at, zl) for at, zl in depth], axis=1),
            jnp.concatenate([gc[at, zl, :, cols] for at, zl in depth], axis=0),
            preferred_element_type=F32,
        )
        value = (C * total + B * ga[mine, :, :, cols].reshape(width, cols.size).astype(F32)).astype(BF16)
        for at, i in enumerate(ORDER):
            pc[(w.y + i) % 4, w.zh, kept_quarter, cols] = value[at * quarter:(at + 1) * quarter]
        gps[n].begin()
        share_p(n, w.fplace(0, 0)).start()

    def take_p(n):
        share_p(n, w.fplace(*gps[n].take())).start()

    def arrived(n, zh):
        for x in range(4):
            share_p(n, (x, zh), True).wait_recv()

    def product(n, zh, first, rows=pl.ds(0, half)):
        cols = columns[n]
        left = jnp.concatenate([xb[j * 2 + zh, rows, :] for j in range(4)], axis=1)
        right = jnp.concatenate([pc[j, zh, :, cols] for j in range(4)], axis=0)
        start = A * xb[mine, rows, cols].astype(F32) if first else acc[rows, cols]
        acc[rows, cols] = start + jnp.dot(left, right, preferred_element_type=F32)

    def back(part):
        rows = pl.ds(part * (half // 2), half // 2)
        return remote(uo.at[rows, :], urecv.at[rows, :], us.at[part], ur.at[part], mate)

    for _ in range(6):
        take_p(0)
        take_p(1)
    gx.take()
    gx.take()
    arrived(0, w.zh)
    product(0, w.zh, True)
    take_p(0)
    arrived(1, w.zh)
    product(1, w.zh, True)
    take_p(1)
    arrived(0, 1 - w.zh)
    product(0, 1 - w.zh, False)
    arrived(1, 1 - w.zh)
    for part in (0, 1):
        rows = pl.ds(part * (half // 2), half // 2)
        product(1, 1 - w.zh, False, rows)
        value = (FACTOR * acc[rows, :]).astype(BF16)
        left, right = value[:, :width], value[:, width:]
        first = c == 0
        uo[rows, :] = jnp.where(first, right, left)
        back(part).start()
        o_ref[pl.ds(pl.multiple_of(c * half + part * (half // 2), 16), half // 2), :] = jnp.where(first, left, right)

    swap.wait_send()
    for g in [gx] + gps + [g for pair in chunks for g in pair]:
        g.end()
    for step in range(8):
        if step in STRAIGHT:
            opposite_copy(step).wait_send()
        for way in (0, 1):
            if step not in STRAIGHT:
                relay_copy(step, way).wait_send()
            x_copy(step, way).wait_send()
    for task in HOPS:
        @pl.when(jnp.logical_not(leaves(task)))
        def _(task=task):
            hop_copy(task).wait_send()

    for i in range(4):
        z_copy(i).wait_send()
    for j in range(8):
        for n in (0, 1):
            share_p(n, (j // 2, j % 2)).wait_send()
        for n in range(2):
            share(n, (j // 2, j % 2)).wait_send()
    for part in (0, 1):
        back(part).wait()
    o_ref[pl.ds((1 - c) * half, half), :] = urecv[...]


def shards(iterate):
    rows, width = iterate.shape
    half, full, quarter = rows // 2, 2 * width, width // 4
    dma = pltpu.SemaphoreType.DMA
    vmem = pltpu.VMEM
    return pl.pallas_call(
        kernel,
        out_shape=jax.ShapeDtypeStruct((rows, width), BF16),
        in_specs=[pl.BlockSpec(memory_space=pl.ANY)],
        out_specs=pl.BlockSpec(memory_space=pltpu.VMEM),
        scratch_shapes=[
            vmem((half, width), BF16),
            vmem((half, width), BF16),
            vmem((8, half, full), BF16),
            vmem((GP, full, full), F32),
            vmem((8, width, full), F32),
            vmem((8, quarter, full), F32),
            vmem((8, width, full), BF16),
            vmem((8, quarter, full), BF16),
            vmem((2, 8, quarter, full), BF16),
            vmem((4, quarter, full), BF16),
            vmem((4, quarter, full), BF16),
            vmem((4, quarter, full), BF16),
            vmem((4, quarter, full), BF16),
            vmem((4, quarter, full), F32),
            vmem((8, 4, quarter, full), BF16),
            vmem((4, 2, full, full), BF16),
            vmem((4, 2, full, full), BF16),
            vmem((half, full), F32),
            vmem((half, width), BF16),
            vmem((half, width), BF16),
            dma((10,)), dma((10,)), dma((4, 9)), dma((4, 9)), dma((4, 9)), dma((4, 9)), dma((2, 8)), dma((2, 8)),
            dma, dma, dma, dma((8,)), dma((8,)), dma((8, 4)), dma((8, 4)), dma((4,)), dma((4,)), dma((4,)), dma((4,)),
            dma((4, 8)), dma((4, 8)), dma((2, 8)), dma((2, 8)), dma((2,)), dma((2,)),
        ],
        compiler_params=pltpu.CompilerParams(
            collective_id=0, has_side_effects=True, vmem_limit_bytes=60 * 2**20
        ),
        cost_estimate=pl.CostEstimate(flops=6 * rows * width * 16 * width, bytes_accessed=4 * rows * width, transcendentals=0),
        name="newton_schulz",
    )(iterate)


def solution(mesh):
    return jax.shard_map(
        shards, mesh=mesh, in_specs=(P("fsdp", "tensor"),), out_specs=P("fsdp", "tensor"), check_vma=False
    )
```

```python
import functools

import jax
import jax.numpy as jnp
from jax import lax
from jax.experimental import pallas as pl
from jax.experimental.pallas import tpu as pltpu
from jax.sharding import PartitionSpec as P

MESH = pl.DeviceIdType.MESH
BF16, F32 = jnp.bfloat16, jnp.float32
ROWS = 12800
FACTOR = 0.2 * ROWS**0.5
A, B, C = 3.4445, -4.775, 2.0315
GP = 4


class Where:
    def __init__(self):
        f, t = lax.axis_index("fsdp"), lax.axis_index("tensor")
        self.zh, self.x = f // 4, f % 4
        self.y, self.zl, self.c = t // 4, (t // 2) % 2, t % 2

    def device(self, dx=0, dzh=0, dy=0, dzl=0, dc=0):
        x, y = (self.x + dx) % 4, (self.y + dy) % 4
        zh, zl, c = (self.zh + dzh) % 2, (self.zl + dzl) % 2, (self.c + dc) % 2
        return (zh * 4 + x, y * 4 + zl * 2 + c)

    def tplace(self, d, dz):
        return (self.y + d) % 4, (self.zl + dz) % 2

    def fplace(self, d, dz):
        return (self.x + d) % 4, (self.zh + dz) % 2


OWN, MINUS, PLUS, OTHER = (0, 0), (-1, 0), (1, 0), (0, 1)
FIRST = {"az": (OWN, (0, 1), None), "ap": (OWN, (1, 0), None), "am": (OWN, (-1, 0), None)}
TWICE = (
    FIRST | {
        "bm": (PLUS, (-1, 0), None), "bz": (PLUS, (0, 1), None), "bp": (OTHER, (1, 0), None),
        "cp": ((-1, 1), (1, 0), 0), "cm": ((1, 1), (-1, 0), 1),
    },
    {"am": ("bm", "bz"), "az": ("bp",), "bp": ("cp",), "bz": ("cm",)},
    [("az",), ("am",), ("ap",), ("bp",), ("bz",), ("bm",), ("cp", "cm")],
)
ONCE = (
    FIRST | {
        "bp": (OTHER, (1, 0), None), "bm": (OTHER, (-1, 0), None), "cp": (MINUS, (1, 0), 0), "cm": (PLUS, (-1, 0), 1),
        "dp": ((-1, 1), (1, 0), 0), "dm": ((1, 1), (-1, 0), 1),
    },
    {"az": ("bp", "bm"), "ap": ("cp",), "am": ("cm",), "bp": ("dp",), "bm": ("dm",)},
    [("az",), ("ap",), ("am",), ("bp",), ("bm",), ("cp", "cm"), ("dp", "dm")],
)
HELD = (
    {name + str(n): (block, way, n) for n in (0, 1) for name, (block, way, _) in FIRST.items()} | {
        "bm": (OTHER, (-1, 0), 0), "bz": (PLUS, (0, 1), 1), "bp": (OTHER, (1, 0), None), "cp": (MINUS, (1, 0), 0),
        "cm": (PLUS, (-1, 0), 1), "dp": ((-1, 1), (1, 0), 0), "dm": ((1, 1), (-1, 0), 1),
    },
    {"az0": ("bm",), "az1": ("bp",), "am1": ("bz",)},
    [("az0", "az1"), ("am0", "am1"), ("ap0", "ap1"), ("bm", "bz"), ("bp",), ("cp", "cm"), ("dp", "dm")],
)
DIRECT = (
    FIRST | {
        "a2": (OWN, (2, 0), None),
        "bp": (OTHER, (1, 0), None), "bm": (OTHER, (-1, 0), None), "b2": (OTHER, (2, 0), None),
    },
    {"az": ("bp", "bm", "b2")},
    [("az",), ("ap",), ("am",), ("a2",), ("bp",), ("bm",), ("b2",)],
)


TASKS = (
    ((0, 0), (0, 0), 0, (0, 0)),
    ((0, 1), (0, 0), 0, (0, 1)),
    ((1, 0), (0, 0), 0, (1, 0)),
    ((0, 1), (1, 0), 1, (-1, 1)),
    ((-1, 0), (0, 0), 0, (-1, 0)),
    ((0, 1), (-1, 0), -1, (1, 1)),
    ((1, 0), (-1, 0), -1, (2, 0)),
    ((1, 1), (-1, 0), -1, (2, 1)),
)
HOPS = (3, 5, 6, 7)
ORDER = (0, 1, 3, 2)
STRAIGHT = (0, 3, 4, 5, 6, 7)


class Gather:
    def __init__(self, way, view, place, device, send, recv):
        self.plan, self.after, self.order = way
        self.view, self.place, self.device, self.send, self.recv = view, place, device, send, recv
        self.names = list(self.plan)
        self.taken = 0

    def copy(self, name, receiving):
        (d, dz), (step, flip), part = self.plan[name]
        if receiving:
            d, dz = d - step, (dz + flip) % 2
        i = self.names.index(name)
        ref = self.view(self.place(d, dz), part)
        return pltpu.make_async_remote_copy(
            src_ref=ref, dst_ref=ref, send_sem=self.send.at[i], recv_sem=self.recv.at[i],
            device_id=self.device(step, flip), device_id_type=MESH,
        )

    def begin(self):
        for name in self.names:
            if name[0] == "a":
                self.copy(name, False).start()

    def take(self):
        names = self.order[self.taken]
        self.taken += 1
        for name in names:
            self.copy(name, True).wait_recv()
            for nxt in self.after.get(name, ()):
                self.copy(nxt, False).start()
        (d, dz), (step, flip), _ = self.plan[names[0]]
        return (d - step + 1) % 4 - 1, (dz + flip) % 2

    def end(self):
        assert self.taken == len(self.order)
        for name in self.names:
            self.copy(name, False).wait_send()


def kernel(
    x_ref, o_ref, xkept, xin, xb, gp, crecv, own, rsst, rlrecv, rsrecv, hopst, hoprecv, rzst, rzrecv, rzown, ga, gc, pc, acc, uo, urecv,
    ts, tr, gs, gr, hs, hr, ps, pr, ks, xs, xr, cs, cr, rss, rsr, hs2, hr2, zs, zr, shs, shr, pss, psr, us, ur,
):
    w = Where()
    c = w.c
    rows, width = x_ref.shape
    half, full, quarter = rows // 2, 2 * width, width // 4
    mate = w.device(dc=1)

    peers = [dict(dc=1), dict(dy=1), dict(dy=-1), dict(dy=2), dict(dzl=1), dict(dx=1), dict(dx=-1), dict(dx=2), dict(dzh=1),
             dict(dy=1, dzh=1), dict(dy=-1, dzh=1)]
    barrier = pltpu.get_barrier_semaphore()
    for peer in peers:
        pl.semaphore_signal(barrier, inc=1, device_id=w.device(**peer), device_id_type=MESH)
    pl.semaphore_wait(barrier, len(peers))

    def remote(src, dst, send, recv, device):
        return pltpu.make_async_remote_copy(
            src_ref=src, dst_ref=dst, send_sem=send, recv_sem=recv, device_id=device, device_id_type=MESH
        )

    part_rows = (half // 32 + 1) * 16
    halves = ((0, part_rows), (part_rows, half - part_rows))

    def swap(n):
        at, size = halves[n]
        return remote(
            x_ref.at[pl.ds((1 - c) * half + at, size), :], xin.at[pl.ds(at, size), :], xs.at[n], xr.at[n], mate
        )

    def keep(n):
        at, size = halves[n]
        return pltpu.make_async_copy(x_ref.at[pl.ds(c * half + at, size), :], xkept.at[pl.ds(at, size), :], ks.at[n])

    for n in (0, 1):
        swap(n).start()
        keep(n).start()
    mine = w.y * 2 + w.zl

    def tdevice(step, flip):
        return w.device(dy=step, dzl=flip)

    def fdevice(step, flip):
        return w.device(dx=step, dzh=flip)

    def slot_of(rel):
        y, zl = w.tplace(*rel)
        return y * 2 + zl

    def xview(place, part):
        at, size = ((0, half), (0, part_rows), (part_rows, half - part_rows))[0 if part is None else part + 1]
        return xb.at[place[0] * 2 + place[1], pl.ds(at, size), :]

    gx = Gather(HELD, xview, w.tplace, tdevice, ts, tr)
    for n, (at, size) in enumerate(halves):
        keep(n).wait()
        swap(n).wait_recv()
        rows = pl.ds(at, size)
        kept, got = xkept[rows, :], xin[rows, :]
        xb[mine, rows, :] = jnp.concatenate([jnp.where(c == 0, kept, got), jnp.where(c == 0, got, kept)], axis=1)
        for name in ("az", "am", "ap"):
            gx.copy(name + str(n), False).start()
    other_rows = pl.ds((1 - c) * width, width)
    kept_rows = pl.ds(c * width, width)
    kept_quarter = pl.ds(c * width + w.x * quarter, quarter)
    done = []

    def gram(task):
        buf = len(done) % GP
        done.append(task)
        j, k = TASKS[task][:2]
        gp[buf] = lax.dot_general(
            xb[slot_of(j)], xb[slot_of(k)], (((0,), (0,)), ((), ())), preferred_element_type=F32
        )
        core_copy(task).start()

    def core_copy(task):
        buf = done.index(task) % GP
        return remote(gp.at[buf, other_rows, :], crecv.at[task], cs.at[task], cr.at[task], mate)

    cut = (quarter // 32 + 1) * 16

    def cuts(task):
        first = cut if task % 2 else quarter - cut
        return (0, first), (first, quarter - first)

    def relay_copy(task, way):
        at, size = cuts(task)[way]
        return remote(
            rsst.at[task, pl.ds((w.x + 2) % 4 * quarter + at, size), :], rlrecv.at[task, pl.ds(at, size), :],
            rss.at[task, way], rsr.at[task, way], w.device(dx=1 - 2 * way),
        )

    def opposite_copy(task):
        return remote(
            rsst.at[task, pl.ds((w.x + 2) % 4 * quarter, quarter), :], rlrecv.at[task],
            rss.at[task, 0], rsr.at[task, 0], w.device(dx=2),
        )

    def x_copy(task, way):
        return remote(
            rsst.at[task, pl.ds((w.x + 1 - 2 * way) % 4 * quarter, quarter), :], rsrecv.at[way, task],
            rss.at[task, 2 + way], rsr.at[task, 2 + way], w.device(dx=1 - 2 * way),
        )

    def hop_copy(task):
        i = HOPS.index(task)
        return remote(hopst.at[i], hoprecv.at[i], hs2.at[i], hr2.at[i], w.device(dy=TASKS[task][2]))

    def z_copy(i, hop=0):
        return remote(rzst.at[i], rzrecv.at[i], zs.at[i], zr.at[i], w.device(dy=hop, dzh=1))

    def leaves(task):
        return (w.zl + TASKS[task][3][1]) % 2 != w.zh

    def scatter(task):
        buf = done.index(task) % GP
        core_copy(task).wait_recv()
        core_copy(task).wait_send()
        own[task] = gp[buf, kept_quarter, :] + crecv[task, pl.ds(w.x * quarter, quarter), :]
        rsst[task] = (gp[buf, kept_rows, :] + crecv[task]).astype(BF16)
        if task in STRAIGHT:
            opposite_copy(task).start()
            for way in (0, 1):
                x_copy(task, way).start()
        else:
            for way in (0, 1):
                relay_copy(task, way).start()

    def relayed(task):
        if task in STRAIGHT:
            return
        for way, (at, size) in enumerate(cuts(task)):
            relay_copy(task, way).wait_recv()
            rows = pl.ds((w.x + 1 - 2 * way) % 4 * quarter + at, size)
            rsst[task, rows, :] = (
                rsst[task, rows, :].astype(F32) + rlrecv[task, pl.ds(at, size), :].astype(F32)
            ).astype(BF16)
            x_copy(task, way).start()

    def summed(task):
        for way in (0, 1):
            x_copy(task, way).wait_recv()
        total = own[task] + rsrecv[0, task].astype(F32) + rsrecv[1, task].astype(F32)
        if task in STRAIGHT:
            opposite_copy(task).wait_recv()
            total += rlrecv[task].astype(F32)
        hop, (i, _) = TASKS[task][2:]
        i = i % 4

        @pl.when(leaves(task))
        def _():
            rzst[i] = total.astype(BF16)
            z_copy(i, hop).start()

        @pl.when(jnp.logical_not(leaves(task)))
        def _():
            if hop:
                hopst[HOPS.index(task)] = total.astype(BF16)
                hop_copy(task).start()
            else:
                rzown[i] = total

    def hopped(task):
        @pl.when(jnp.logical_not(leaves(task)))
        def _():
            hop_copy(task).wait_recv()
            rzown[TASKS[task][3][0] % 4] = hoprecv[HOPS.index(task)].astype(F32)

    def chunk(n, way_f, way_t):
        def which(half_of):
            return pl.ds(2 * n, 2) if half_of is None else pl.ds(2 * n + half_of, 1)

        def cview(place, half_of):
            return gc.at[which(half_of), place[1], pl.ds(c * width + place[0] * quarter, quarter), :]

        def aview(place, half_of):
            return ga.at[place[0] * 2 + place[1], which(half_of)]

        return (
            Gather(way_f, cview, w.fplace, fdevice, gs.at[n], gr.at[n]),
            Gather(way_t, aview, w.tplace, tdevice, hs.at[n], hr.at[n]),
        )

    chunks = (chunk(0, ONCE, TWICE), chunk(1, ONCE, TWICE))

    def share(n, place, other=False):
        x, zh = place
        core = 1 - c if other else c
        ref = gc.at[pl.ds(2 * n, 2), zh, pl.ds(core * width + x * quarter, quarter), :]
        return remote(ref, ref, shs.at[n, x * 2 + zh], shr.at[n, x * 2 + zh], mate)

    def ready(i):
        z_copy(i).wait_recv()
        block = (rzown[i] + rzrecv[i].astype(F32)).astype(BF16)
        at = ORDER.index(i)
        ga[mine, at] = block
        gc[at, w.zh, kept_quarter, :] = block

    def begin(n):
        for g in chunks[n]:
            g.begin()
        share(n, w.fplace(0, 0)).start()

    def take_f(n, count):
        for _ in range(count):
            share(n, w.fplace(*chunks[n][0].take())).start()

    def take_t(n, count):
        for _ in range(count):
            chunks[n][1].take()

    gram(0)
    scatter(0)
    summed(0)
    for _ in range(3):
        gx.take()
    gram(1)
    gram(2)
    scatter(1)
    gram(5)
    scatter(2)
    gram(4)
    relayed(1)
    scatter(5)
    gram(3)
    relayed(2)
    scatter(4)
    gram(6)
    scatter(3)
    scatter(6)
    for _ in range(1):
        gx.take()
    gram(7)
    scatter(7)
    summed(1)
    summed(2)
    summed(5)
    ready(0)
    hopped(5)
    ready(1)
    begin(0)
    summed(4)
    summed(3)
    summed(6)
    hopped(3)
    ready(3)
    summed(7)
    take_f(0, 3)
    hopped(6)
    hopped(7)
    ready(2)
    begin(1)
    take_t(0, 3)
    take_f(1, 3)
    take_t(1, 3)
    take_f(0, 2)
    take_t(0, 2)
    take_f(1, 2)
    take_t(1, 2)
    take_f(0, 2)
    take_t(0, 2)
    take_f(1, 2)
    take_t(1, 2)
    for _ in range(1):
        gx.take()
    for name in ("cp", "cm", "dp", "dm"):
        gx.copy(name, False).start()
    for n in range(2):
        for j in range(8):
            share(n, (j // 2, j % 2), True).wait_recv()

    columns = [pl.ds(at, min(384, full - at)) for at in range(0, full, 384)]

    def pview(cols):
        def view(place, half_of):
            which = pl.ds(0, 4) if half_of is None else pl.ds(2 * half_of, 2)
            return pc.at[which, place[1], pl.ds(c * width + place[0] * quarter, quarter), cols]

        return view

    def share_p(n, place, other=False):
        x, zh = place
        core = 1 - c if other else c
        ref = pc.at[:, zh, pl.ds(core * width + x * quarter, quarter), columns[n]]
        return remote(ref, ref, pss.at[n, x * 2 + zh], psr.at[n, x * 2 + zh], mate)

    gps = [Gather(TWICE, pview(cols), w.fplace, fdevice, ps.at[n], pr.at[n]) for n, cols in enumerate(columns)]
    def rows_of(at, zl):
        slot = (w.y + ORDER[at]) % 4 * 2 + zl
        return jnp.concatenate([ga[slot, ORDER.index((i - ORDER[at]) % 4)] for i in ORDER], axis=0)

    depth = [(at, zl) for at in range(4) for zl in range(2)]
    for n, cols in enumerate(columns):
        total = jnp.dot(
            jnp.concatenate([rows_of(at, zl) for at, zl in depth], axis=1),
            jnp.concatenate([gc[at, zl, :, cols] for at, zl in depth], axis=0),
            preferred_element_type=F32,
        )
        value = (C * total + B * ga[mine, :, :, cols].reshape(width, cols.size).astype(F32)).astype(BF16)
        for at, i in enumerate(ORDER):
            pc[(w.y + i) % 4, w.zh, kept_quarter, cols] = value[at * quarter:(at + 1) * quarter]
        gps[n].begin()
        share_p(n, w.fplace(0, 0)).start()

    def take_p(n):
        share_p(n, w.fplace(*gps[n].take())).start()

    def arrived(n, zh):
        for x in range(4):
            share_p(n, (x, zh), True).wait_recv()

    def product(n, zh, first, rows=pl.ds(0, half)):
        cols = columns[n]
        left = jnp.concatenate([xb[j * 2 + zh, rows, :] for j in range(4)], axis=1)
        right = jnp.concatenate([pc[j, zh, :, cols] for j in range(4)], axis=0)
        start = A * xb[mine, rows, cols].astype(F32) if first else acc[rows, cols]
        acc[rows, cols] = start + jnp.dot(left, right, preferred_element_type=F32)

    def back(part):
        rows = pl.ds(part * (half // 2), half // 2)
        return remote(uo.at[rows, :], urecv.at[rows, :], us.at[part], ur.at[part], mate)

    for _ in range(6):
        take_p(0)
        take_p(1)
    gx.take()
    gx.take()
    arrived(0, w.zh)
    product(0, w.zh, True)
    take_p(0)
    arrived(1, w.zh)
    product(1, w.zh, True)
    take_p(1)
    arrived(0, 1 - w.zh)
    product(0, 1 - w.zh, False)
    arrived(1, 1 - w.zh)
    for part in (0, 1):
        rows = pl.ds(part * (half // 2), half // 2)
        product(1, 1 - w.zh, False, rows)
        value = (FACTOR * acc[rows, :]).astype(BF16)
        left, right = value[:, :width], value[:, width:]
        first = c == 0
        uo[rows, :] = jnp.where(first, right, left)
        back(part).start()
        o_ref[pl.ds(pl.multiple_of(c * half + part * (half // 2), 16), half // 2), :] = jnp.where(first, left, right)

    for n in (0, 1):
        swap(n).wait_send()
    for g in [gx] + gps + [g for pair in chunks for g in pair]:
        g.end()
    for step in range(8):
        if step in STRAIGHT:
            opposite_copy(step).wait_send()
        for way in (0, 1):
            if step not in STRAIGHT:
                relay_copy(step, way).wait_send()
            x_copy(step, way).wait_send()
    for task in HOPS:
        @pl.when(jnp.logical_not(leaves(task)))
        def _(task=task):
            hop_copy(task).wait_send()

    for i in range(4):
        z_copy(i).wait_send()
    for j in range(8):
        for n in (0, 1):
            share_p(n, (j // 2, j % 2)).wait_send()
        for n in range(2):
            share(n, (j // 2, j % 2)).wait_send()
    for part in (0, 1):
        back(part).wait()
    o_ref[pl.ds((1 - c) * half, half), :] = urecv[...]


def shards(iterate):
    rows, width = iterate.shape
    half, full, quarter = rows // 2, 2 * width, width // 4
    dma = pltpu.SemaphoreType.DMA
    vmem = pltpu.VMEM
    return pl.pallas_call(
        kernel,
        out_shape=jax.ShapeDtypeStruct((rows, width), BF16),
        in_specs=[pl.BlockSpec(memory_space=pl.ANY)],
        out_specs=pl.BlockSpec(memory_space=pltpu.VMEM),
        scratch_shapes=[
            vmem((half, width), BF16),
            vmem((half, width), BF16),
            vmem((8, half, full), BF16),
            vmem((GP, full, full), F32),
            vmem((8, width, full), F32),
            vmem((8, quarter, full), F32),
            vmem((8, width, full), BF16),
            vmem((8, quarter, full), BF16),
            vmem((2, 8, quarter, full), BF16),
            vmem((4, quarter, full), BF16),
            vmem((4, quarter, full), BF16),
            vmem((4, quarter, full), BF16),
            vmem((4, quarter, full), BF16),
            vmem((4, quarter, full), F32),
            vmem((8, 4, quarter, full), BF16),
            vmem((4, 2, full, full), BF16),
            vmem((4, 2, full, full), BF16),
            vmem((half, full), F32),
            vmem((half, width), BF16),
            vmem((half, width), BF16),
            dma((13,)), dma((13,)), dma((4, 9)), dma((4, 9)), dma((4, 9)), dma((4, 9)), dma((2, 8)), dma((2, 8)),
            dma((2,)), dma((2,)), dma((2,)), dma((8,)), dma((8,)), dma((8, 4)), dma((8, 4)), dma((4,)), dma((4,)), dma((4,)), dma((4,)),
            dma((4, 8)), dma((4, 8)), dma((2, 8)), dma((2, 8)), dma((2,)), dma((2,)),
        ],
        compiler_params=pltpu.CompilerParams(
            collective_id=0, has_side_effects=True, vmem_limit_bytes=60 * 2**20
        ),
        cost_estimate=pl.CostEstimate(flops=6 * rows * width * 16 * width, bytes_accessed=4 * rows * width, transcendentals=0),
        name="newton_schulz",
    )(iterate)


def solution(mesh):
    return jax.shard_map(
        shards, mesh=mesh, in_specs=(P("fsdp", "tensor"),), out_specs=P("fsdp", "tensor"), check_vma=False
    )
```

```python
import functools

import jax
import jax.numpy as jnp
from jax import lax
from jax.experimental import pallas as pl
from jax.experimental.pallas import tpu as pltpu
from jax.sharding import PartitionSpec as P

MESH = pl.DeviceIdType.MESH
BF16, F32 = jnp.bfloat16, jnp.float32
ROWS = 12800
FACTOR = 0.2 * ROWS**0.5
A, B, C = 3.4445, -4.775, 2.0315
GP = 4


class Where:
    def __init__(self):
        f, t = lax.axis_index("fsdp"), lax.axis_index("tensor")
        self.zh, self.x = f // 4, f % 4
        self.y, self.zl, self.c = t // 4, (t // 2) % 2, t % 2

    def device(self, dx=0, dzh=0, dy=0, dzl=0, dc=0):
        x, y = (self.x + dx) % 4, (self.y + dy) % 4
        zh, zl, c = (self.zh + dzh) % 2, (self.zl + dzl) % 2, (self.c + dc) % 2
        return (zh * 4 + x, y * 4 + zl * 2 + c)

    def tplace(self, d, dz):
        return (self.y + d) % 4, (self.zl + dz) % 2

    def fplace(self, d, dz):
        return (self.x + d) % 4, (self.zh + dz) % 2


OWN, MINUS, PLUS, OTHER = (0, 0), (-1, 0), (1, 0), (0, 1)
FIRST = {"az": (OWN, (0, 1), None), "ap": (OWN, (1, 0), None), "am": (OWN, (-1, 0), None)}
TWICE = (
    FIRST | {
        "bm": (PLUS, (-1, 0), None), "bz": (PLUS, (0, 1), None), "bp": (OTHER, (1, 0), None),
        "cp": ((-1, 1), (1, 0), 0), "cm": ((1, 1), (-1, 0), 1),
    },
    {"am": ("bm", "bz"), "az": ("bp",), "bp": ("cp",), "bz": ("cm",)},
    [("az",), ("am",), ("ap",), ("bp",), ("bz",), ("bm",), ("cp", "cm")],
)
ONCE = (
    FIRST | {
        "bp": (OTHER, (1, 0), None), "bm": (OTHER, (-1, 0), None), "cp": (MINUS, (1, 0), 0), "cm": (PLUS, (-1, 0), 1),
        "dp": ((-1, 1), (1, 0), 0), "dm": ((1, 1), (-1, 0), 1),
    },
    {"az": ("bp", "bm"), "ap": ("cp",), "am": ("cm",), "bp": ("dp",), "bm": ("dm",)},
    [("az",), ("ap",), ("am",), ("bp",), ("bm",), ("cp", "cm"), ("dp", "dm")],
)
HELD = (
    {name + str(n): (block, way, n) for n in (0, 1) for name, (block, way, _) in FIRST.items()} | {
        "bm": (OTHER, (-1, 0), 0), "bz": (PLUS, (0, 1), 1), "bp": (OTHER, (1, 0), None), "cp": (MINUS, (1, 0), 0),
        "cm": (PLUS, (-1, 0), 1), "dp": ((-1, 1), (1, 0), 0), "dm": ((1, 1), (-1, 0), 1),
    },
    {"az0": ("bm",), "az1": ("bp",), "am1": ("bz",)},
    [("az0", "az1"), ("am0", "am1"), ("ap0", "ap1"), ("bm", "bz"), ("bp",), ("cp", "cm"), ("dp", "dm")],
)
DIRECT = (
    FIRST | {
        "a2": (OWN, (2, 0), None),
        "bp": (OTHER, (1, 0), None), "bm": (OTHER, (-1, 0), None), "b2": (OTHER, (2, 0), None),
    },
    {"az": ("bp", "bm", "b2")},
    [("az",), ("ap",), ("am",), ("a2",), ("bp",), ("bm",), ("b2",)],
)


TASKS = (
    ((0, 0), (0, 0), 0, (0, 0)),
    ((0, 1), (0, 0), 0, (0, 1)),
    ((1, 0), (0, 0), 0, (1, 0)),
    ((0, 1), (1, 0), 1, (-1, 1)),
    ((-1, 0), (0, 0), 0, (-1, 0)),
    ((0, 1), (-1, 0), -1, (1, 1)),
    ((1, 0), (-1, 0), -1, (2, 0)),
    ((1, 1), (-1, 0), -1, (2, 1)),
)
HOPS = (3, 5, 6, 7)
ORDER = (0, 1, 3, 2)
STRAIGHT = (0, 3, 4, 5, 6, 7)


class Gather:
    def __init__(self, way, view, place, device, send, recv):
        self.plan, self.after, self.order = way
        self.view, self.place, self.device, self.send, self.recv = view, place, device, send, recv
        self.names = list(self.plan)
        self.taken = 0

    def copy(self, name, receiving):
        (d, dz), (step, flip), part = self.plan[name]
        if receiving:
            d, dz = d - step, (dz + flip) % 2
        i = self.names.index(name)
        ref = self.view(self.place(d, dz), part)
        return pltpu.make_async_remote_copy(
            src_ref=ref, dst_ref=ref, send_sem=self.send.at[i], recv_sem=self.recv.at[i],
            device_id=self.device(step, flip), device_id_type=MESH,
        )

    def begin(self):
        for name in self.names:
            if name[0] == "a":
                self.copy(name, False).start()

    def take(self):
        names = self.order[self.taken]
        self.taken += 1
        for name in names:
            self.copy(name, True).wait_recv()
            for nxt in self.after.get(name, ()):
                self.copy(nxt, False).start()
        (d, dz), (step, flip), _ = self.plan[names[0]]
        return (d - step + 1) % 4 - 1, (dz + flip) % 2

    def end(self):
        assert self.taken == len(self.order)
        for name in self.names:
            self.copy(name, False).wait_send()


def kernel(
    x_ref, o_ref, xkept, xin, xb, gp, crecv, own, rsst, rlrecv, rsrecv, hopst, hoprecv, rzst, rzrecv, rzown, ga, gc, pc, acc, uo, urecv,
    ts, tr, gs, gr, hs, hr, ps, pr, ks, xs, xr, cs, cr, rss, rsr, hs2, hr2, zs, zr, shs, shr, pss, psr, us, ur,
):
    w = Where()
    c = w.c
    rows, width = x_ref.shape
    half, full, quarter = rows // 2, 2 * width, width // 4
    mate = w.device(dc=1)

    peers = [dict(dc=1), dict(dy=1), dict(dy=-1), dict(dy=2), dict(dzl=1), dict(dx=1), dict(dx=-1), dict(dx=2), dict(dzh=1),
             dict(dy=1, dzh=1), dict(dy=-1, dzh=1)]
    barrier = pltpu.get_barrier_semaphore()
    for peer in peers:
        pl.semaphore_signal(barrier, inc=1, device_id=w.device(**peer), device_id_type=MESH)
    pl.semaphore_wait(barrier, len(peers))

    def remote(src, dst, send, recv, device):
        return pltpu.make_async_remote_copy(
            src_ref=src, dst_ref=dst, send_sem=send, recv_sem=recv, device_id=device, device_id_type=MESH
        )

    part_rows = (half // 32 + 1) * 16
    halves = ((0, part_rows), (part_rows, half - part_rows))

    def swap(n):
        at, size = halves[n]
        return remote(
            x_ref.at[pl.ds((1 - c) * half + at, size), :], xin.at[pl.ds(at, size), :], xs.at[n], xr.at[n], mate
        )

    def keep(n):
        at, size = halves[n]
        return pltpu.make_async_copy(x_ref.at[pl.ds(c * half + at, size), :], xkept.at[pl.ds(at, size), :], ks.at[n])

    for n in (0, 1):
        swap(n).start()
        keep(n).start()
    mine = w.y * 2 + w.zl

    def tdevice(step, flip):
        return w.device(dy=step, dzl=flip)

    def fdevice(step, flip):
        return w.device(dx=step, dzh=flip)

    def slot_of(rel):
        y, zl = w.tplace(*rel)
        return y * 2 + zl

    def xview(place, part):
        at, size = ((0, half), (0, part_rows), (part_rows, half - part_rows))[0 if part is None else part + 1]
        return xb.at[place[0] * 2 + place[1], pl.ds(at, size), :]

    gx = Gather(HELD, xview, w.tplace, tdevice, ts, tr)
    for n, (at, size) in enumerate(halves):
        keep(n).wait()
        swap(n).wait_recv()
        rows = pl.ds(at, size)
        kept, got = xkept[rows, :], xin[rows, :]
        xb[mine, rows, :] = jnp.concatenate([jnp.where(c == 0, kept, got), jnp.where(c == 0, got, kept)], axis=1)
        for name in ("az", "am", "ap"):
            gx.copy(name + str(n), False).start()
    other_rows = pl.ds((1 - c) * width, width)
    kept_rows = pl.ds(c * width, width)
    kept_quarter = pl.ds(c * width + w.x * quarter, quarter)
    done = []

    def gram(task):
        buf = len(done) % GP
        done.append(task)
        j, k = TASKS[task][:2]
        gp[buf] = lax.dot_general(
            xb[slot_of(j)], xb[slot_of(k)], (((0,), (0,)), ((), ())), preferred_element_type=F32
        )
        core_copy(task).start()

    def core_copy(task):
        buf = done.index(task) % GP
        return remote(gp.at[buf, other_rows, :], crecv.at[task], cs.at[task], cr.at[task], mate)

    cut = (quarter // 32 + 1) * 16

    def cuts(task):
        first = cut if task % 2 else quarter - cut
        return (0, first), (first, quarter - first)

    def relay_copy(task, way):
        at, size = cuts(task)[way]
        return remote(
            rsst.at[task, pl.ds((w.x + 2) % 4 * quarter + at, size), :], rlrecv.at[task, pl.ds(at, size), :],
            rss.at[task, way], rsr.at[task, way], w.device(dx=1 - 2 * way),
        )

    def opposite_copy(task):
        return remote(
            rsst.at[task, pl.ds((w.x + 2) % 4 * quarter, quarter), :], rlrecv.at[task],
            rss.at[task, 0], rsr.at[task, 0], w.device(dx=2),
        )

    def x_copy(task, way):
        return remote(
            rsst.at[task, pl.ds((w.x + 1 - 2 * way) % 4 * quarter, quarter), :], rsrecv.at[way, task],
            rss.at[task, 2 + way], rsr.at[task, 2 + way], w.device(dx=1 - 2 * way),
        )

    def hop_copy(task):
        i = HOPS.index(task)
        return remote(hopst.at[i], hoprecv.at[i], hs2.at[i], hr2.at[i], w.device(dy=TASKS[task][2]))

    def z_copy(i, hop=0):
        return remote(rzst.at[i], rzrecv.at[i], zs.at[i], zr.at[i], w.device(dy=hop, dzh=1))

    def leaves(task):
        return (w.zl + TASKS[task][3][1]) % 2 != w.zh

    def scatter(task):
        buf = done.index(task) % GP
        core_copy(task).wait_recv()
        core_copy(task).wait_send()
        own[task] = gp[buf, kept_quarter, :] + crecv[task, pl.ds(w.x * quarter, quarter), :]
        rsst[task] = (gp[buf, kept_rows, :] + crecv[task]).astype(BF16)
        if task in STRAIGHT:
            opposite_copy(task).start()
            for way in (0, 1):
                x_copy(task, way).start()
        else:
            for way in (0, 1):
                relay_copy(task, way).start()

    def relayed(task):
        if task in STRAIGHT:
            return
        for way, (at, size) in enumerate(cuts(task)):
            relay_copy(task, way).wait_recv()
            rows = pl.ds((w.x + 1 - 2 * way) % 4 * quarter + at, size)
            rsst[task, rows, :] = (
                rsst[task, rows, :].astype(F32) + rlrecv[task, pl.ds(at, size), :].astype(F32)
            ).astype(BF16)
            x_copy(task, way).start()

    def summed(task):
        for way in (0, 1):
            x_copy(task, way).wait_recv()
        total = own[task] + rsrecv[0, task].astype(F32) + rsrecv[1, task].astype(F32)
        if task in STRAIGHT:
            opposite_copy(task).wait_recv()
            total += rlrecv[task].astype(F32)
        hop, (i, _) = TASKS[task][2:]
        i = i % 4

        @pl.when(leaves(task))
        def _():
            rzst[i] = total.astype(BF16)
            z_copy(i, hop).start()

        @pl.when(jnp.logical_not(leaves(task)))
        def _():
            if hop:
                hopst[HOPS.index(task)] = total.astype(BF16)
                hop_copy(task).start()
            else:
                rzown[i] = total

    def hopped(task):
        @pl.when(jnp.logical_not(leaves(task)))
        def _():
            hop_copy(task).wait_recv()
            rzown[TASKS[task][3][0] % 4] = hoprecv[HOPS.index(task)].astype(F32)

    def chunk(n, way_f, way_t):
        def which(half_of):
            return pl.ds(2 * n, 2) if half_of is None else pl.ds(2 * n + half_of, 1)

        def cview(place, half_of):
            return gc.at[which(half_of), place[1], pl.ds(c * width + place[0] * quarter, quarter), :]

        def aview(place, half_of):
            return ga.at[place[0] * 2 + place[1], which(half_of)]

        return (
            Gather(way_f, cview, w.fplace, fdevice, gs.at[n], gr.at[n]),
            Gather(way_t, aview, w.tplace, tdevice, hs.at[n], hr.at[n]),
        )

    chunks = (chunk(0, ONCE, TWICE), chunk(1, ONCE, TWICE))

    def share(n, place, other=False):
        x, zh = place
        core = 1 - c if other else c
        ref = gc.at[pl.ds(2 * n, 2), zh, pl.ds(core * width + x * quarter, quarter), :]
        return remote(ref, ref, shs.at[n, x * 2 + zh], shr.at[n, x * 2 + zh], mate)

    def ready(i):
        z_copy(i).wait_recv()
        block = (rzown[i] + rzrecv[i].astype(F32)).astype(BF16)
        at = ORDER.index(i)
        ga[mine, at] = block
        gc[at, w.zh, kept_quarter, :] = block

    def begin(n):
        for g in chunks[n]:
            g.begin()
        share(n, w.fplace(0, 0)).start()

    def take_f(n, count):
        for _ in range(count):
            share(n, w.fplace(*chunks[n][0].take())).start()

    def take_t(n, count):
        for _ in range(count):
            chunks[n][1].take()

    gram(0)
    scatter(0)
    summed(0)
    for _ in range(3):
        gx.take()
    gram(1)
    gram(2)
    scatter(1)
    gram(5)
    scatter(2)
    gram(4)
    relayed(1)
    scatter(5)
    gram(3)
    relayed(2)
    scatter(4)
    gram(6)
    scatter(3)
    scatter(6)
    for _ in range(1):
        gx.take()
    gram(7)
    scatter(7)
    summed(1)
    summed(2)
    summed(5)
    ready(0)
    hopped(5)
    ready(1)
    begin(0)
    summed(4)
    summed(3)
    summed(6)
    hopped(3)
    ready(3)
    summed(7)
    take_f(0, 3)
    hopped(6)
    hopped(7)
    ready(2)
    begin(1)
    take_t(0, 3)
    take_f(1, 3)
    take_t(1, 3)
    take_f(0, 2)
    take_t(0, 2)
    take_f(1, 2)
    take_t(1, 2)
    for _ in range(1):
        gx.take()
    for name in ("cp", "cm", "dp", "dm"):
        gx.copy(name, False).start()
    take_f(0, 2)
    take_t(0, 2)
    take_f(1, 2)
    take_t(1, 2)
    for n in range(2):
        for j in range(8):
            share(n, (j // 2, j % 2), True).wait_recv()

    columns = [pl.ds(at, min(384, full - at)) for at in range(0, full, 384)]

    def pview(cols):
        def view(place, half_of):
            which = pl.ds(0, 4) if half_of is None else pl.ds(2 * half_of, 2)
            return pc.at[which, place[1], pl.ds(c * width + place[0] * quarter, quarter), cols]

        return view

    def share_p(n, place, other=False):
        x, zh = place
        core = 1 - c if other else c
        ref = pc.at[:, zh, pl.ds(core * width + x * quarter, quarter), columns[n]]
        return remote(ref, ref, pss.at[n, x * 2 + zh], psr.at[n, x * 2 + zh], mate)

    gps = [Gather(TWICE, pview(cols), w.fplace, fdevice, ps.at[n], pr.at[n]) for n, cols in enumerate(columns)]
    def rows_of(at, zl):
        slot = (w.y + ORDER[at]) % 4 * 2 + zl
        return jnp.concatenate([ga[slot, ORDER.index((i - ORDER[at]) % 4)] for i in ORDER], axis=0)

    depth = [(at, zl) for at in range(4) for zl in range(2)]
    for n, cols in enumerate(columns):
        total = jnp.dot(
            jnp.concatenate([rows_of(at, zl) for at, zl in depth], axis=1),
            jnp.concatenate([gc[at, zl, :, cols] for at, zl in depth], axis=0),
            preferred_element_type=F32,
        )
        value = (C * total + B * ga[mine, :, :, cols].reshape(width, cols.size).astype(F32)).astype(BF16)
        for at, i in enumerate(ORDER):
            pc[(w.y + i) % 4, w.zh, kept_quarter, cols] = value[at * quarter:(at + 1) * quarter]
        gps[n].begin()
        share_p(n, w.fplace(0, 0)).start()

    def take_p(n):
        share_p(n, w.fplace(*gps[n].take())).start()

    def arrived(n, zh):
        for x in range(4):
            share_p(n, (x, zh), True).wait_recv()

    def product(n, zh, first, rows=pl.ds(0, half)):
        cols = columns[n]
        left = jnp.concatenate([xb[j * 2 + zh, rows, :] for j in range(4)], axis=1)
        right = jnp.concatenate([pc[j, zh, :, cols] for j in range(4)], axis=0)
        start = A * xb[mine, rows, cols].astype(F32) if first else acc[rows, cols]
        acc[rows, cols] = start + jnp.dot(left, right, preferred_element_type=F32)

    def back(part):
        rows = pl.ds(part * (half // 2), half // 2)
        return remote(uo.at[rows, :], urecv.at[rows, :], us.at[part], ur.at[part], mate)

    for _ in range(6):
        take_p(0)
        take_p(1)
    gx.take()
    gx.take()
    arrived(0, w.zh)
    product(0, w.zh, True)
    take_p(0)
    arrived(1, w.zh)
    product(1, w.zh, True)
    take_p(1)
    arrived(0, 1 - w.zh)
    product(0, 1 - w.zh, False)
    arrived(1, 1 - w.zh)
    for part in (0, 1):
        rows = pl.ds(part * (half // 2), half // 2)
        product(1, 1 - w.zh, False, rows)
        value = (FACTOR * acc[rows, :]).astype(BF16)
        left, right = value[:, :width], value[:, width:]
        first = c == 0
        uo[rows, :] = jnp.where(first, right, left)
        back(part).start()
        o_ref[pl.ds(pl.multiple_of(c * half + part * (half // 2), 16), half // 2), :] = jnp.where(first, left, right)

    for n in (0, 1):
        swap(n).wait_send()
    for g in [gx] + gps + [g for pair in chunks for g in pair]:
        g.end()
    for step in range(8):
        if step in STRAIGHT:
            opposite_copy(step).wait_send()
        for way in (0, 1):
            if step not in STRAIGHT:
                relay_copy(step, way).wait_send()
            x_copy(step, way).wait_send()
    for task in HOPS:
        @pl.when(jnp.logical_not(leaves(task)))
        def _(task=task):
            hop_copy(task).wait_send()

    for i in range(4):
        z_copy(i).wait_send()
    for j in range(8):
        for n in (0, 1):
            share_p(n, (j // 2, j % 2)).wait_send()
        for n in range(2):
            share(n, (j // 2, j % 2)).wait_send()
    for part in (0, 1):
        back(part).wait()
    o_ref[pl.ds((1 - c) * half, half), :] = urecv[...]


def shards(iterate):
    rows, width = iterate.shape
    half, full, quarter = rows // 2, 2 * width, width // 4
    dma = pltpu.SemaphoreType.DMA
    vmem = pltpu.VMEM
    return pl.pallas_call(
        kernel,
        out_shape=jax.ShapeDtypeStruct((rows, width), BF16),
        in_specs=[pl.BlockSpec(memory_space=pl.ANY)],
        out_specs=pl.BlockSpec(memory_space=pltpu.VMEM),
        scratch_shapes=[
            vmem((half, width), BF16),
            vmem((half, width), BF16),
            vmem((8, half, full), BF16),
            vmem((GP, full, full), F32),
            vmem((8, width, full), F32),
            vmem((8, quarter, full), F32),
            vmem((8, width, full), BF16),
            vmem((8, quarter, full), BF16),
            vmem((2, 8, quarter, full), BF16),
            vmem((4, quarter, full), BF16),
            vmem((4, quarter, full), BF16),
            vmem((4, quarter, full), BF16),
            vmem((4, quarter, full), BF16),
            vmem((4, quarter, full), F32),
            vmem((8, 4, quarter, full), BF16),
            vmem((4, 2, full, full), BF16),
            vmem((4, 2, full, full), BF16),
            vmem((half, full), F32),
            vmem((half, width), BF16),
            vmem((half, width), BF16),
            dma((13,)), dma((13,)), dma((4, 9)), dma((4, 9)), dma((4, 9)), dma((4, 9)), dma((2, 8)), dma((2, 8)),
            dma((2,)), dma((2,)), dma((2,)), dma((8,)), dma((8,)), dma((8, 4)), dma((8, 4)), dma((4,)), dma((4,)), dma((4,)), dma((4,)),
            dma((4, 8)), dma((4, 8)), dma((2, 8)), dma((2, 8)), dma((2,)), dma((2,)),
        ],
        compiler_params=pltpu.CompilerParams(
            collective_id=0, has_side_effects=True, vmem_limit_bytes=60 * 2**20
        ),
        cost_estimate=pl.CostEstimate(flops=6 * rows * width * 16 * width, bytes_accessed=4 * rows * width, transcendentals=0),
        name="newton_schulz",
    )(iterate)


def solution(mesh):
    return jax.shard_map(
        shards, mesh=mesh, in_specs=(P("fsdp", "tensor"),), out_specs=P("fsdp", "tensor"), check_vma=False
    )
```

```python
import functools

import jax
import jax.numpy as jnp
from jax import lax
from jax.experimental import pallas as pl
from jax.experimental.pallas import tpu as pltpu
from jax.sharding import PartitionSpec as P

MESH = pl.DeviceIdType.MESH
BF16, F32 = jnp.bfloat16, jnp.float32
ROWS = 12800
FACTOR = 0.2 * ROWS**0.5
A, B, C = 3.4445, -4.775, 2.0315
GP = 4


class Where:
    def __init__(self):
        f, t = lax.axis_index("fsdp"), lax.axis_index("tensor")
        self.zh, self.x = f // 4, f % 4
        self.y, self.zl, self.c = t // 4, (t // 2) % 2, t % 2

    def device(self, dx=0, dzh=0, dy=0, dzl=0, dc=0):
        x, y = (self.x + dx) % 4, (self.y + dy) % 4
        zh, zl, c = (self.zh + dzh) % 2, (self.zl + dzl) % 2, (self.c + dc) % 2
        return (zh * 4 + x, y * 4 + zl * 2 + c)

    def tplace(self, d, dz):
        return (self.y + d) % 4, (self.zl + dz) % 2

    def fplace(self, d, dz):
        return (self.x + d) % 4, (self.zh + dz) % 2


OWN, MINUS, PLUS, OTHER = (0, 0), (-1, 0), (1, 0), (0, 1)
FIRST = {"az": (OWN, (0, 1), None), "ap": (OWN, (1, 0), None), "am": (OWN, (-1, 0), None)}
TWICE = (
    FIRST | {
        "bm": (PLUS, (-1, 0), None), "bz": (PLUS, (0, 1), None), "bp": (OTHER, (1, 0), None),
        "cp": ((-1, 1), (1, 0), 0), "cm": ((1, 1), (-1, 0), 1),
    },
    {"am": ("bm", "bz"), "az": ("bp",), "bp": ("cp",), "bz": ("cm",)},
    [("az",), ("am",), ("ap",), ("bp",), ("bz",), ("bm",), ("cp", "cm")],
)
ONCE = (
    FIRST | {
        "bp": (OTHER, (1, 0), None), "bm": (OTHER, (-1, 0), None), "cp": (MINUS, (1, 0), 0), "cm": (PLUS, (-1, 0), 1),
        "dp": ((-1, 1), (1, 0), 0), "dm": ((1, 1), (-1, 0), 1),
    },
    {"az": ("bp", "bm"), "ap": ("cp",), "am": ("cm",), "bp": ("dp",), "bm": ("dm",)},
    [("az",), ("ap",), ("am",), ("bp",), ("bm",), ("cp", "cm"), ("dp", "dm")],
)
HELD = (
    {name + str(n): (block, way, n) for n in (0, 1) for name, (block, way, _) in FIRST.items()} | {
        "bm": (OTHER, (-1, 0), 0), "bz": (PLUS, (0, 1), 1), "bp": (OTHER, (1, 0), None), "cp": (MINUS, (1, 0), 0),
        "cm": (PLUS, (-1, 0), 1), "dp": ((-1, 1), (1, 0), 0), "dm": ((1, 1), (-1, 0), 1),
    },
    {"az0": ("bm",), "az1": ("bp",), "am1": ("bz",)},
    [("az0", "az1"), ("am0", "am1"), ("ap0", "ap1"), ("bm", "bz"), ("bp",), ("cp", "cm"), ("dp", "dm")],
)
DIRECT = (
    FIRST | {
        "a2": (OWN, (2, 0), None),
        "bp": (OTHER, (1, 0), None), "bm": (OTHER, (-1, 0), None), "b2": (OTHER, (2, 0), None),
    },
    {"az": ("bp", "bm", "b2")},
    [("az",), ("ap",), ("am",), ("a2",), ("bp",), ("bm",), ("b2",)],
)


TASKS = (
    ((0, 0), (0, 0), 0, (0, 0)),
    ((0, 1), (0, 0), 0, (0, 1)),
    ((1, 0), (0, 0), 0, (1, 0)),
    ((0, 1), (1, 0), 1, (-1, 1)),
    ((-1, 0), (0, 0), 0, (-1, 0)),
    ((0, 1), (-1, 0), -1, (1, 1)),
    ((1, 0), (-1, 0), -1, (2, 0)),
    ((1, 1), (-1, 0), -1, (2, 1)),
)
HOPS = (3, 5, 6, 7)
ORDER = (0, 1, 3, 2)
STRAIGHT = (0, 3, 4, 5, 6, 7)


class Gather:
    def __init__(self, way, view, place, device, send, recv):
        self.plan, self.after, self.order = way
        self.view, self.place, self.device, self.send, self.recv = view, place, device, send, recv
        self.names = list(self.plan)
        self.taken = 0

    def copy(self, name, receiving):
        (d, dz), (step, flip), part = self.plan[name]
        if receiving:
            d, dz = d - step, (dz + flip) % 2
        i = self.names.index(name)
        ref = self.view(self.place(d, dz), part)
        return pltpu.make_async_remote_copy(
            src_ref=ref, dst_ref=ref, send_sem=self.send.at[i], recv_sem=self.recv.at[i],
            device_id=self.device(step, flip), device_id_type=MESH,
        )

    def begin(self):
        for name in self.names:
            if name[0] == "a":
                self.copy(name, False).start()

    def take(self):
        names = self.order[self.taken]
        self.taken += 1
        for name in names:
            self.copy(name, True).wait_recv()
            for nxt in self.after.get(name, ()):
                self.copy(nxt, False).start()
        (d, dz), (step, flip), _ = self.plan[names[0]]
        return (d - step + 1) % 4 - 1, (dz + flip) % 2

    def end(self):
        assert self.taken == len(self.order)
        for name in self.names:
            self.copy(name, False).wait_send()


def kernel(
    x_ref, o_ref, xkept, xin, xb, gp, crecv, csend, own, rsst, rlrecv, rsrecv, hopst, hoprecv, rzst, rzrecv, rzown, ga, gc, pc, acc, uo, urecv,
    ts, tr, gs, gr, hs, hr, ps, pr, ks, xs, xr, cs, cr, rss, rsr, hs2, hr2, zs, zr, shs, shr, pss, psr, us, ur,
):
    w = Where()
    c = w.c
    rows, width = x_ref.shape
    half, full, quarter = rows // 2, 2 * width, width // 4
    mate = w.device(dc=1)

    peers = [dict(dc=1), dict(dy=1), dict(dy=-1), dict(dy=2), dict(dzl=1), dict(dx=1), dict(dx=-1), dict(dx=2), dict(dzh=1),
             dict(dy=1, dzh=1), dict(dy=-1, dzh=1)]
    barrier = pltpu.get_barrier_semaphore()
    for peer in peers:
        pl.semaphore_signal(barrier, inc=1, device_id=w.device(**peer), device_id_type=MESH)
    pl.semaphore_wait(barrier, len(peers))

    def remote(src, dst, send, recv, device):
        return pltpu.make_async_remote_copy(
            src_ref=src, dst_ref=dst, send_sem=send, recv_sem=recv, device_id=device, device_id_type=MESH
        )

    part_rows = (half // 32 + 1) * 16
    halves = ((0, part_rows), (part_rows, half - part_rows))

    def swap(n):
        at, size = halves[n]
        return remote(
            x_ref.at[pl.ds((1 - c) * half + at, size), :], xin.at[pl.ds(at, size), :], xs.at[n], xr.at[n], mate
        )

    def keep(n):
        at, size = halves[n]
        return pltpu.make_async_copy(x_ref.at[pl.ds(c * half + at, size), :], xkept.at[pl.ds(at, size), :], ks.at[n])

    for n in (0, 1):
        swap(n).start()
        keep(n).start()
    mine = w.y * 2 + w.zl

    def tdevice(step, flip):
        return w.device(dy=step, dzl=flip)

    def fdevice(step, flip):
        return w.device(dx=step, dzh=flip)

    def slot_of(rel):
        y, zl = w.tplace(*rel)
        return y * 2 + zl

    def xview(place, part):
        at, size = ((0, half), (0, part_rows), (part_rows, half - part_rows))[0 if part is None else part + 1]
        return xb.at[place[0] * 2 + place[1], pl.ds(at, size), :]

    gx = Gather(HELD, xview, w.tplace, tdevice, ts, tr)
    for n, (at, size) in enumerate(halves):
        keep(n).wait()
        swap(n).wait_recv()
        rows = pl.ds(at, size)
        kept, got = xkept[rows, :], xin[rows, :]
        xb[mine, rows, :] = jnp.concatenate([jnp.where(c == 0, kept, got), jnp.where(c == 0, got, kept)], axis=1)
        for name in ("az", "am", "ap"):
            gx.copy(name + str(n), False).start()
    other_rows = pl.ds((1 - c) * width, width)
    kept_rows = pl.ds(c * width, width)
    kept_quarter = pl.ds(c * width + w.x * quarter, quarter)
    done = []

    def gram(task):
        buf = len(done) % GP
        done.append(task)
        j, k = TASKS[task][:2]
        gp[buf] = lax.dot_general(
            xb[slot_of(j)], xb[slot_of(k)], (((0,), (0,)), ((), ())), preferred_element_type=F32
        )
        csend[buf] = gp[buf, other_rows, :].astype(BF16)
        core_copy(task).start()

    def core_copy(task):
        buf = done.index(task) % GP
        return remote(csend.at[buf], crecv.at[task], cs.at[task], cr.at[task], mate)

    cut = (quarter // 32 + 1) * 16

    def cuts(task):
        first = cut if task % 2 else quarter - cut
        return (0, first), (first, quarter - first)

    def relay_copy(task, way):
        at, size = cuts(task)[way]
        return remote(
            rsst.at[task, pl.ds((w.x + 2) % 4 * quarter + at, size), :], rlrecv.at[task, pl.ds(at, size), :],
            rss.at[task, way], rsr.at[task, way], w.device(dx=1 - 2 * way),
        )

    def opposite_copy(task):
        return remote(
            rsst.at[task, pl.ds((w.x + 2) % 4 * quarter, quarter), :], rlrecv.at[task],
            rss.at[task, 0], rsr.at[task, 0], w.device(dx=2),
        )

    def x_copy(task, way):
        return remote(
            rsst.at[task, pl.ds((w.x + 1 - 2 * way) % 4 * quarter, quarter), :], rsrecv.at[way, task],
            rss.at[task, 2 + way], rsr.at[task, 2 + way], w.device(dx=1 - 2 * way),
        )

    def hop_copy(task):
        i = HOPS.index(task)
        return remote(hopst.at[i], hoprecv.at[i], hs2.at[i], hr2.at[i], w.device(dy=TASKS[task][2]))

    def z_copy(i, hop=0):
        return remote(rzst.at[i], rzrecv.at[i], zs.at[i], zr.at[i], w.device(dy=hop, dzh=1))

    def leaves(task):
        return (w.zl + TASKS[task][3][1]) % 2 != w.zh

    def scatter(task):
        buf = done.index(task) % GP
        core_copy(task).wait_recv()
        core_copy(task).wait_send()
        own[task] = gp[buf, kept_quarter, :] + crecv[task, pl.ds(w.x * quarter, quarter), :].astype(F32)
        rsst[task] = (gp[buf, kept_rows, :] + crecv[task].astype(F32)).astype(BF16)
        if task in STRAIGHT:
            opposite_copy(task).start()
            for way in (0, 1):
                x_copy(task, way).start()
        else:
            for way in (0, 1):
                relay_copy(task, way).start()

    def relayed(task):
        if task in STRAIGHT:
            return
        for way, (at, size) in enumerate(cuts(task)):
            relay_copy(task, way).wait_recv()
            rows = pl.ds((w.x + 1 - 2 * way) % 4 * quarter + at, size)
            rsst[task, rows, :] = (
                rsst[task, rows, :].astype(F32) + rlrecv[task, pl.ds(at, size), :].astype(F32)
            ).astype(BF16)
            x_copy(task, way).start()

    def summed(task):
        for way in (0, 1):
            x_copy(task, way).wait_recv()
        total = own[task] + rsrecv[0, task].astype(F32) + rsrecv[1, task].astype(F32)
        if task in STRAIGHT:
            opposite_copy(task).wait_recv()
            total += rlrecv[task].astype(F32)
        hop, (i, _) = TASKS[task][2:]
        i = i % 4

        @pl.when(leaves(task))
        def _():
            rzst[i] = total.astype(BF16)
            z_copy(i, hop).start()

        @pl.when(jnp.logical_not(leaves(task)))
        def _():
            if hop:
                hopst[HOPS.index(task)] = total.astype(BF16)
                hop_copy(task).start()
            else:
                rzown[i] = total

    def hopped(task):
        @pl.when(jnp.logical_not(leaves(task)))
        def _():
            hop_copy(task).wait_recv()
            rzown[TASKS[task][3][0] % 4] = hoprecv[HOPS.index(task)].astype(F32)

    def chunk(n, way_f, way_t):
        def which(half_of):
            return pl.ds(2 * n, 2) if half_of is None else pl.ds(2 * n + half_of, 1)

        def cview(place, half_of):
            return gc.at[which(half_of), place[1], pl.ds(c * width + place[0] * quarter, quarter), :]

        def aview(place, half_of):
            return ga.at[place[0] * 2 + place[1], which(half_of)]

        return (
            Gather(way_f, cview, w.fplace, fdevice, gs.at[n], gr.at[n]),
            Gather(way_t, aview, w.tplace, tdevice, hs.at[n], hr.at[n]),
        )

    chunks = (chunk(0, ONCE, TWICE), chunk(1, ONCE, TWICE))

    def share(n, place, other=False):
        x, zh = place
        core = 1 - c if other else c
        ref = gc.at[pl.ds(2 * n, 2), zh, pl.ds(core * width + x * quarter, quarter), :]
        return remote(ref, ref, shs.at[n, x * 2 + zh], shr.at[n, x * 2 + zh], mate)

    def ready(i):
        z_copy(i).wait_recv()
        block = (rzown[i] + rzrecv[i].astype(F32)).astype(BF16)
        at = ORDER.index(i)
        ga[mine, at] = block
        gc[at, w.zh, kept_quarter, :] = block

    def begin(n):
        for g in chunks[n]:
            g.begin()
        share(n, w.fplace(0, 0)).start()

    def take_f(n, count):
        for _ in range(count):
            share(n, w.fplace(*chunks[n][0].take())).start()

    def take_t(n, count):
        for _ in range(count):
            chunks[n][1].take()

    gram(0)
    scatter(0)
    summed(0)
    for _ in range(3):
        gx.take()
    gram(1)
    gram(2)
    scatter(1)
    gram(5)
    scatter(2)
    gram(4)
    relayed(1)
    scatter(5)
    gram(3)
    relayed(2)
    scatter(4)
    gram(6)
    scatter(3)
    scatter(6)
    for _ in range(1):
        gx.take()
    gram(7)
    scatter(7)
    summed(1)
    summed(2)
    summed(5)
    ready(0)
    hopped(5)
    ready(1)
    begin(0)
    summed(4)
    summed(3)
    summed(6)
    hopped(3)
    ready(3)
    summed(7)
    take_f(0, 3)
    hopped(6)
    hopped(7)
    ready(2)
    begin(1)
    take_t(0, 3)
    take_f(1, 3)
    take_t(1, 3)
    take_f(0, 2)
    take_t(0, 2)
    take_f(1, 2)
    take_t(1, 2)
    take_f(0, 2)
    take_t(0, 2)
    take_f(1, 2)
    take_t(1, 2)
    for _ in range(1):
        gx.take()
    for name in ("cp", "cm", "dp", "dm"):
        gx.copy(name, False).start()
    for n in range(2):
        for j in range(8):
            share(n, (j // 2, j % 2), True).wait_recv()

    columns = [pl.ds(at, min(384, full - at)) for at in range(0, full, 384)]

    def pview(cols):
        def view(place, half_of):
            which = pl.ds(0, 4) if half_of is None else pl.ds(2 * half_of, 2)
            return pc.at[which, place[1], pl.ds(c * width + place[0] * quarter, quarter), cols]

        return view

    def share_p(n, place, other=False):
        x, zh = place
        core = 1 - c if other else c
        ref = pc.at[:, zh, pl.ds(core * width + x * quarter, quarter), columns[n]]
        return remote(ref, ref, pss.at[n, x * 2 + zh], psr.at[n, x * 2 + zh], mate)

    gps = [Gather(TWICE, pview(cols), w.fplace, fdevice, ps.at[n], pr.at[n]) for n, cols in enumerate(columns)]
    def rows_of(at, zl):
        slot = (w.y + ORDER[at]) % 4 * 2 + zl
        return jnp.concatenate([ga[slot, ORDER.index((i - ORDER[at]) % 4)] for i in ORDER], axis=0)

    depth = [(at, zl) for at in range(4) for zl in range(2)]
    for n, cols in enumerate(columns):
        total = jnp.dot(
            jnp.concatenate([rows_of(at, zl) for at, zl in depth], axis=1),
            jnp.concatenate([gc[at, zl, :, cols] for at, zl in depth], axis=0),
            preferred_element_type=F32,
        )
        value = (C * total + B * ga[mine, :, :, cols].reshape(width, cols.size).astype(F32)).astype(BF16)
        for at, i in enumerate(ORDER):
            pc[(w.y + i) % 4, w.zh, kept_quarter, cols] = value[at * quarter:(at + 1) * quarter]
        gps[n].begin()
        share_p(n, w.fplace(0, 0)).start()

    def take_p(n):
        share_p(n, w.fplace(*gps[n].take())).start()

    def arrived(n, zh):
        for x in range(4):
            share_p(n, (x, zh), True).wait_recv()

    def product(n, zh, first, rows=pl.ds(0, half)):
        cols = columns[n]
        left = jnp.concatenate([xb[j * 2 + zh, rows, :] for j in range(4)], axis=1)
        right = jnp.concatenate([pc[j, zh, :, cols] for j in range(4)], axis=0)
        start = A * xb[mine, rows, cols].astype(F32) if first else acc[rows, cols]
        acc[rows, cols] = start + jnp.dot(left, right, preferred_element_type=F32)

    def back(part):
        rows = pl.ds(part * (half // 2), half // 2)
        return remote(uo.at[rows, :], urecv.at[rows, :], us.at[part], ur.at[part], mate)

    for _ in range(6):
        take_p(0)
        take_p(1)
    gx.take()
    gx.take()
    arrived(0, w.zh)
    product(0, w.zh, True)
    take_p(0)
    arrived(1, w.zh)
    product(1, w.zh, True)
    take_p(1)
    arrived(0, 1 - w.zh)
    product(0, 1 - w.zh, False)
    arrived(1, 1 - w.zh)
    for part in (0, 1):
        rows = pl.ds(part * (half // 2), half // 2)
        product(1, 1 - w.zh, False, rows)
        value = (FACTOR * acc[rows, :]).astype(BF16)
        left, right = value[:, :width], value[:, width:]
        first = c == 0
        uo[rows, :] = jnp.where(first, right, left)
        back(part).start()
        o_ref[pl.ds(pl.multiple_of(c * half + part * (half // 2), 16), half // 2), :] = jnp.where(first, left, right)

    for n in (0, 1):
        swap(n).wait_send()
    for g in [gx] + gps + [g for pair in chunks for g in pair]:
        g.end()
    for step in range(8):
        if step in STRAIGHT:
            opposite_copy(step).wait_send()
        for way in (0, 1):
            if step not in STRAIGHT:
                relay_copy(step, way).wait_send()
            x_copy(step, way).wait_send()
    for task in HOPS:
        @pl.when(jnp.logical_not(leaves(task)))
        def _(task=task):
            hop_copy(task).wait_send()

    for i in range(4):
        z_copy(i).wait_send()
    for j in range(8):
        for n in (0, 1):
            share_p(n, (j // 2, j % 2)).wait_send()
        for n in range(2):
            share(n, (j // 2, j % 2)).wait_send()
    for part in (0, 1):
        back(part).wait()
    o_ref[pl.ds((1 - c) * half, half), :] = urecv[...]


def shards(iterate):
    rows, width = iterate.shape
    half, full, quarter = rows // 2, 2 * width, width // 4
    dma = pltpu.SemaphoreType.DMA
    vmem = pltpu.VMEM
    return pl.pallas_call(
        kernel,
        out_shape=jax.ShapeDtypeStruct((rows, width), BF16),
        in_specs=[pl.BlockSpec(memory_space=pl.ANY)],
        out_specs=pl.BlockSpec(memory_space=pltpu.VMEM),
        scratch_shapes=[
            vmem((half, width), BF16),
            vmem((half, width), BF16),
            vmem((8, half, full), BF16),
            vmem((GP, full, full), F32),
            vmem((8, width, full), BF16),
            vmem((GP, width, full), BF16),
            vmem((8, quarter, full), F32),
            vmem((8, width, full), BF16),
            vmem((8, quarter, full), BF16),
            vmem((2, 8, quarter, full), BF16),
            vmem((4, quarter, full), BF16),
            vmem((4, quarter, full), BF16),
            vmem((4, quarter, full), BF16),
            vmem((4, quarter, full), BF16),
            vmem((4, quarter, full), F32),
            vmem((8, 4, quarter, full), BF16),
            vmem((4, 2, full, full), BF16),
            vmem((4, 2, full, full), BF16),
            vmem((half, full), F32),
            vmem((half, width), BF16),
            vmem((half, width), BF16),
            dma((13,)), dma((13,)), dma((4, 9)), dma((4, 9)), dma((4, 9)), dma((4, 9)), dma((2, 8)), dma((2, 8)),
            dma((2,)), dma((2,)), dma((2,)), dma((8,)), dma((8,)), dma((8, 4)), dma((8, 4)), dma((4,)), dma((4,)), dma((4,)), dma((4,)),
            dma((4, 8)), dma((4, 8)), dma((2, 8)), dma((2, 8)), dma((2,)), dma((2,)),
        ],
        compiler_params=pltpu.CompilerParams(
            collective_id=0, has_side_effects=True, vmem_limit_bytes=60 * 2**20
        ),
        cost_estimate=pl.CostEstimate(flops=6 * rows * width * 16 * width, bytes_accessed=4 * rows * width, transcendentals=0),
        name="newton_schulz",
    )(iterate)


def solution(mesh):
    return jax.shard_map(
        shards, mesh=mesh, in_specs=(P("fsdp", "tensor"),), out_specs=P("fsdp", "tensor"), check_vma=False
    )
```
